512 devices in a mesh: dp: 32 (over z, core), tensor: 16 (over x, y).
Axes of the slice: x: 4, y: 4, z: 16, core: 2. Of those that a mesh axis runs over, the one named last changes fastest.
Arguments:
- activations: bfloat16 [32768, 1024], P('dp'), may hold values from -6 to 6
- out_grads: bfloat16 [32768, 4096], P('dp', 'tensor'), may hold values from -0.1875 to 0.1875
- q_previous: float32 [64, 4096], P(None, 'tensor'), may hold values from -0.09375 to 0.09375
- carried_error: float32 [32, 1024, 4096], P('dp', None, 'tensor'), may hold values from -12 to 12
Outputs:
- q_factor: float32 [64, 4096], P(None, 'tensor')
- new_residual: float32 [32, 1024, 4096], P('dp', None, 'tensor')
The draws below stay inside these ranges and needn't reach their ends.
All inputs are finite; a program needn't handle non-finite values.
Results may differ from the reference program's by a relative error of at most 0.0003.
Values sent between devices are 32-bit elements; how exact they have to be, the bound alone decides.
A program may use at most 64 MiB of HBM per device.

```python
import math
import jax
import jax.numpy as jnp
from jax import lax

FF = 4096
ROWS = 1024
TOK = 1024
RANK = 64
REPLICAS = 32
TOKENS = 32768


def draw_carried_error(key, part):
    key = jax.random.fold_in(key, 7)
    key_scale = jax.random.fold_in(key, 0)
    key_own = jax.random.fold_in(key, 2)
    low_end = math.log(0.3)
    high_end = math.log(3.0)
    scales = jnp.exp(jax.random.uniform(key_scale, (REPLICAS, ROWS, 1), jnp.float32, low_end, high_end))
    own = jax.random.truncated_normal(key_own, -4.0, 4.0, (REPLICAS, ROWS, FF), jnp.float32)
    return (scales * own).astype(jnp.float32)


def spiked(entries, own_key, source, target, blocks, factor):
    def block_of(axis_at):
        return (jnp.arange(entries.shape[axis_at]) // (entries.shape[axis_at] // blocks)).reshape((-1,) + (1,) * (entries.ndim - 1 - axis_at))

    first = jax.random.permutation(own_key, blocks)[block_of(target)]
    far = (block_of(target) + blocks // 2) % blocks
    return jnp.where((block_of(source) == first) | (block_of(source) == far), factor * entries, entries)


def levels(key, extent, shards, low, largest):
    level, own = 1.0, jax.random.fold_in(key, 6)
    for axis_at, shards_of in shards:
        heights = jnp.exp(jax.random.uniform(jax.random.fold_in(own, axis_at), (shards_of,), jnp.float32, low / len(shards), largest / len(shards)))
        level = level * jnp.repeat(heights, extent[axis_at] // shards_of).reshape([-1 if axis == axis_at else 1 for axis in range(len(extent))])
    return level


def gaussian(key, shape, deviation, limit, pieces=(), held_as=jnp.bfloat16):
    entries = jax.random.normal(key, shape, jnp.float32) * deviation
    if len(pieces) > 0:
        entries = levels(key, shape, pieces, -0.22, 0.18) * entries
    return jnp.clip(entries, min=-limit, max=limit).astype(held_as)


def heavy_noise(own_key, dims, spread, limit, cuts, heavy, kind=jnp.bfloat16):
    entries = spread * jax.random.normal(own_key, dims, jnp.float32)
    if cuts:
        entries = entries * levels(own_key, dims, cuts, -0.22, 0.18)
    return jnp.clip(spiked(entries, jax.random.fold_in(own_key, 3), *heavy), -limit, limit).astype(kind)


def setup_inputs(seed: int = 0) -> dict:
    arg_keys = jax.random.split(jax.random.key(seed), 5)
    return {
        "activations": heavy_noise(arg_keys[0], (TOKENS, ROWS), 1.0, 6.0, ((0, 32),), (0, 1, 32, 2.75)),
        "out_grads": gaussian(arg_keys[1], (TOKENS, FF), TOK ** -0.5, 0.1875, ((0, 32), (1, 16))),
        "q_previous": gaussian(arg_keys[2], (RANK, FF), FF ** -0.5, 0.09375, ((1, 16),), jnp.float32),
        "carried_error": draw_carried_error(jax.random.fold_in(arg_keys[4], 71), 0),
    }


ridge_scale = 0.001
highest = lax.Precision.HIGHEST

def orthonormal(p_sum):
    gram_matrix = lax.dot_general(p_sum.astype(jnp.float32), p_sum.astype(jnp.float32), (((0,), (0,)), ((), ())), precision=highest, preferred_element_type=jnp.float32)
    ridge_shift = ridge_scale * ROWS * (jnp.trace(gram_matrix) / (ROWS * RANK) + 1e-05)
    factor = jnp.linalg.cholesky(gram_matrix + ridge_shift * jnp.eye(RANK, dtype=jnp.float32))
    return jax.scipy.linalg.solve_triangular(factor, p_sum.T, lower=True).T

def reference(activations, out_grads, q_previous, carried_error):
    acts_split = activations.reshape(REPLICAS, TOK, ROWS)
    grads_split = out_grads.reshape(REPLICAS, TOK, FF)

    def form(triple):
        left, right, carried = triple
        return lax.dot_general(left.astype(jnp.float32), right.astype(jnp.float32), (((0,), (0,)), ((), ())), preferred_element_type=jnp.float32) + carried
    merged = lax.map(form, (acts_split, grads_split, carried_error))

    def add_left(total, member):
        return (total + lax.dot_general(member.astype(jnp.float32), q_previous.astype(jnp.float32), (((1,), (1,)), ((), ())), precision=highest, preferred_element_type=jnp.float32), None)
    p_sum, _ = lax.scan(add_left, jnp.zeros((ROWS, RANK), jnp.float32), merged)
    spanning = orthonormal(p_sum)

    def add_right(total, member):
        return (total + lax.dot_general(spanning.astype(jnp.float32), member.astype(jnp.float32), (((0,), (0,)), ((), ())), precision=highest, preferred_element_type=jnp.float32), None)
    q_total, _ = lax.scan(add_right, jnp.zeros((RANK, FF), jnp.float32), merged)
    q_factor = q_total / REPLICAS
    low_rank = jnp.dot(spanning.astype(jnp.float32), q_factor.astype(jnp.float32), precision=highest, preferred_element_type=jnp.float32)
    new_residual = merged - low_rank[None]
    return (q_factor, new_residual)
```

```python
import functools

import jax
import jax.numpy as jnp
from jax import lax
from jax.experimental import pallas as pl
from jax.experimental.pallas import tpu as pltpu
from jax.sharding import PartitionSpec as P

ridge_scale = 0.001
highest = lax.Precision.HIGHEST
f32 = jnp.float32
bf16 = jnp.bfloat16
MESH = pl.DeviceIdType.MESH
CORES = 2


def dot(a, b, ca, cb, precision=None):
    return lax.dot_general(
        a, b, (((ca,), (cb,)), ((), ())), precision=precision, preferred_element_type=f32
    )


def split(value):
    high = value.astype(bf16)
    return high, (value - high.astype(f32)).astype(bf16)


def dot3(a, b, ca, cb):
    return dot(a[0], b[0], ca, cb) + (dot(a[0], b[1], ca, cb) + dot(a[1], b[0], ca, cb))


def await_bytes(ref, sem):
    pltpu.make_async_copy(ref, ref, sem).wait()


def ring_order(n):
    return sorted(range(1, n), key=lambda k: -min(k, n - k))


def kernel(
    nx, ny, nz,
    act_hbm, grad_hbm, q_hbm, err_hbm, factor_ref, res_hbm,
    act, grads, q_prev, err, merged, part, from_core, half, xy_in, z_out, z_in, p_t,
    n_own, pair_in, cross_out, cross_in, n_all, res,
    load_sem, core_send, core_recv, xy_send, xy_recv, z_send, z_recv, ag_send, ag_recv,
    fw_send, fw_recv, pair_send, pair_recv, cross_send, cross_recv, back_send, back_recv, out_sem,
):
    rank, rows = p_t.shape
    nt = nx * ny
    hrank = rank // CORES
    crank = hrank // nx
    width = rows // ny
    quarter = rank // 4
    npair = nz // 2

    dp, t = lax.axis_index("dp"), lax.axis_index("tensor")
    z, c = lax.div(dp, CORES), lax.rem(dp, CORES)
    x, y = lax.div(t, ny), lax.rem(t, ny)

    def device(z_at, c_at, x_at, y_at):
        return {"dp": z_at * CORES + c_at, "tensor": x_at * ny + y_at}

    def around(at, step, n):
        return lax.rem(at + step, n)

    def send(src, dst, send_sem, recv_sem, to):
        pltpu.make_async_remote_copy(
            src_ref=src, dst_ref=dst, send_sem=send_sem, recv_sem=recv_sem,
            device_id=to, device_id_type=MESH,
        ).start()

    sibling = device(z, 1 - c, x, y)
    plane = sorted(
        ((dx, dy) for dx in range(nx) for dy in range(ny) if dx or dy),
        key=lambda d: -(min(d[0], nx - d[0]) + min(d[1], ny - d[1])),
    )
    ring = ring_order(nz)
    mate = z + 1 - 2 * lax.rem(z, 2)

    block_order = ring_order(ny) + [0]

    def columns(offset):
        return pl.ds(pl.multiple_of(around(y, offset, ny) * width, width), width)

    loads = [
        [pltpu.make_async_copy(grad_hbm, grads, load_sem.at[0]),
         pltpu.make_async_copy(q_hbm, q_prev, load_sem.at[1])]
    ]
    for k, offset in enumerate(block_order):
        at = columns(offset)
        loads.append([
            pltpu.make_async_copy(act_hbm.at[:, at], act.at[:, at], load_sem.at[2 + 2 * k]),
            pltpu.make_async_copy(err_hbm.at[0, at, :], err.at[at, :], load_sem.at[3 + 2 * k]),
        ])
    for group in loads:
        for copy in group:
            copy.start()

    barrier = pltpu.get_barrier_semaphore()
    greeted = [sibling, device(mate, 1 - c, x, y)]
    greeted += [device(z, c, around(x, dx, nx), around(y, dy, ny)) for dx, dy in plane]
    greeted += [device(around(z, dz, nz), c, x, y) for dz in ring]
    for other in greeted:
        pl.semaphore_signal(barrier, inc=1, device_id=other, device_id_type=MESH)

    own_half = pl.ds(pl.multiple_of(c * hrank, hrank), hrank)
    other_half = pl.ds(pl.multiple_of((1 - c) * hrank, hrank), hrank)

    def scatter(k, offset):
        at = columns(offset)
        await_bytes(from_core.at[k], core_recv.at[k])
        half[k] = part[own_half, at] + from_core[k]
        for dx in ring_order(nx) + [0]:
            to_x = around(x, dx, nx)
            mine = pl.ds(pl.multiple_of(to_x * crank, crank), crank)
            if dx == 0 and offset == 0:
                xy_in[t] = half[k, mine, :]
            else:
                send(half.at[k, mine, :], xy_in.at[t], xy_send, xy_recv,
                     device(z, c, to_x, around(y, offset, ny)))

    for copy in loads[0]:
        copy.wait()
    q_split = split(q_prev[...])
    for k, offset in enumerate(block_order):
        at = columns(offset)
        for copy in loads[1 + k]:
            copy.wait()
        block = dot(act[:, at], grads[...], 0, 0) + err[at, :]
        merged[at, :] = block
        part[:, at] = dot3(q_split, split(block), 1, 1)
        if k == 0:
            pl.semaphore_wait(barrier, len(greeted))
        send(part.at[other_half, at], from_core.at[k], core_send, core_recv.at[k], sibling)
        if k > 0:
            scatter(k - 1, block_order[k - 1])
    scatter(ny - 1, block_order[-1])

    await_bytes(xy_in.at[pl.ds(0, nt - 1)], xy_recv)
    piece = jnp.sum(xy_in[...], axis=0)
    z_out[...] = piece
    for dz in ring:
        send(z_out, z_in.at[z], z_send, z_recv, device(around(z, dz, nz), c, x, y))
    z_in[z] = piece
    await_bytes(z_in.at[pl.ds(0, nz - 1)], z_recv)
    my_rows = pl.ds(pl.multiple_of(c * hrank + x * crank, crank), crank)
    my_piece = p_t.at[my_rows, columns(0)]
    my_piece[...] = jnp.sum(z_in[...], axis=0)

    for dx, dy in plane:
        send(my_piece, my_piece, ag_send, ag_recv.at[(ny - dy) % ny],
             device(z, c, around(x, dx, nx), around(y, dy, ny)))
    near_first = list(reversed(block_order))
    for offset in near_first:
        count = (nx - 1 if offset == 0 else nx) * crank
        await_bytes(p_t.at[pl.ds(0, count), pl.ds(0, width)], ag_recv.at[offset])
        piece_ref = p_t.at[own_half, columns(offset)]
        send(piece_ref, piece_ref, fw_send, fw_recv.at[offset], sibling)
    total = None
    for offset in near_first:
        at = columns(offset)
        await_bytes(p_t.at[pl.ds(0, hrank), pl.ds(0, width)], fw_recv.at[offset])
        term = dot3(split(p_t[:, at]), split(merged[at, :]), 1, 0)
        total = term if total is None else total + term
    n_own[...] = total

    place = lax.rem(z, 2) * CORES + c

    def rows_of(at):
        return pl.ds(pl.multiple_of(at * quarter, quarter), quarter)

    group = [(mate, 1 - c), (mate, c), (z, 1 - c)]
    for z_at, c_at in group:
        there = lax.rem(z_at, 2) * CORES + c_at
        send(n_own.at[rows_of(there), :], pair_in.at[place], pair_send, pair_recv,
             device(z_at, c_at, x, y))
    pair_in[place] = n_own[rows_of(place), :]

    gram = dot(p_t[...], p_t[...], 1, 1, highest)
    row_at = lax.broadcasted_iota(jnp.int32, (rank, rank), 0)
    col_at = lax.broadcasted_iota(jnp.int32, (rank, rank), 1)
    eye = jnp.where(row_at == col_at, 1.0, 0.0).astype(f32)
    trace = jnp.sum(jnp.sum(gram * eye, axis=1, keepdims=True), axis=0, keepdims=True)
    shift = ridge_scale * rows * (trace / (rows * rank) + 1e-05)
    both = jnp.concatenate([gram + shift * eye, eye], axis=1)
    rank_at = lax.broadcasted_iota(jnp.int32, (rank, 1), 0)

    def eliminate(table, pivots, first, last):
        for k in range(first, last):
            pivot = table[k : k + 1, k : k + 1]
            pivots = jnp.where(rank_at == k, pivot, pivots)
            scale = jnp.where(rank_at > k, table[:, k : k + 1] * (1.0 / pivot), 0.0)
            table = table - scale * table[k : k + 1, :]
        return table, pivots

    early = rank // 4
    both, pivots = eliminate(both, jnp.ones((rank, 1), f32), 0, early)

    await_bytes(pair_in.at[pl.ds(0, 3)], pair_recv)
    piece = jnp.sum(pair_in[...], axis=0)
    cross_out[...] = piece
    pair_at = lax.div(z, 2)
    for dz in ring:
        if dz % 2 == 0:
            send(cross_out, cross_in.at[pair_at], cross_send, cross_recv,
                 device(around(z, dz, nz), c, x, y))
    cross_in[pair_at] = piece

    both, pivots = eliminate(both, pivots, early, rank)
    inverse = both[:, rank:] * (1.0 / jnp.sqrt(pivots))

    await_bytes(cross_in.at[pl.ds(0, npair - 1)], cross_recv)
    mine = n_all.at[rows_of(place), :]
    mine[...] = jnp.sum(cross_in[...], axis=0)
    for z_at, c_at in group:
        send(mine, mine, back_send, back_recv, device(z_at, c_at, x, y))
    await_bytes(n_all.at[pl.ds(0, 3 * quarter), :], back_recv)

    factor = dot(inverse, n_all[...], 1, 0, highest) * (1.0 / (nz * CORES))
    factor_ref[...] = factor
    back = split(dot(inverse, factor, 0, 0, highest))
    outs = []
    for offset in near_first:
        at = columns(offset)
        res[at, :] = merged[at, :] - dot3(split(p_t[:, at].T), back, 1, 0)
        outs.append(pltpu.make_async_copy(res.at[at, :], res_hbm.at[0, at, :], out_sem.at[offset]))
        outs[-1].start()

    await_bytes(from_core, core_send)
    await_bytes(xy_in.at[pl.ds(0, nt - 1)], xy_send)
    await_bytes(z_in.at[pl.ds(0, nz - 1)], z_send)
    await_bytes(xy_in.at[pl.ds(0, nt - 1)], ag_send)
    await_bytes(from_core, fw_send)
    await_bytes(pair_in.at[pl.ds(0, 3)], pair_send)
    await_bytes(cross_in.at[pl.ds(0, npair - 1)], cross_send)
    await_bytes(pair_in.at[pl.ds(0, 3)], back_send)
    for copy in outs:
        copy.wait()


def on_device(nx, ny, nz, activations, out_grads, q_previous, carried_error):
    tokens, rows = activations.shape
    width = out_grads.shape[1]
    rank = q_previous.shape[0]
    nt = nx * ny
    piece = (rank // CORES // nx, rows // ny)
    quarter = (rank // 4, width)
    vmem, dma = pltpu.VMEM, pltpu.SemaphoreType.DMA
    anywhere = pl.BlockSpec(memory_space=pl.ANY)
    factor, residual = pl.pallas_call(
        functools.partial(kernel, nx, ny, nz),
        name="powersgd",
        out_shape=(
            jax.ShapeDtypeStruct((rank, width), f32),
            jax.ShapeDtypeStruct((1, rows, width), f32),
        ),
        in_specs=[anywhere] * 4,
        out_specs=(pl.BlockSpec(memory_space=pltpu.VMEM), anywhere),
        scratch_shapes=[
            vmem((tokens, rows), bf16),
            vmem((tokens, width), bf16),
            vmem((rank, width), f32),
            vmem((rows, width), f32),
            vmem((rows, width), f32),
            vmem((rank, rows), f32),
            vmem((ny, rank // CORES, rows // ny), f32),
            vmem((ny, rank // CORES, rows // ny), f32),
            vmem((nt, *piece), f32),
            vmem(piece, f32),
            vmem((nz, *piece), f32),
            vmem((rank, rows), f32),
            vmem((rank, width), f32),
            vmem((4, *quarter), f32),
            vmem(quarter, f32),
            vmem((nz // 2, *quarter), f32),
            vmem((rank, width), f32),
            vmem((rows, width), f32),
            dma((2 + 2 * ny,)),
            dma, dma((ny,)),
            dma, dma,
            dma, dma,
            dma, dma((ny,)),
            dma, dma((ny,)),
            dma, dma,
            dma, dma,
            dma, dma,
            dma((ny,)),
        ],
        compiler_params=pltpu.CompilerParams(
            collective_id=0, has_side_effects=True, vmem_limit_bytes=32 * 1024 * 1024
        ),
    )(activations, out_grads, q_previous, carried_error)
    return factor, residual


def solution(mesh):
    nz = mesh.shape["dp"] // CORES
    nx = ny = {16: 4, 4: 2}[mesh.shape["tensor"]]
    placed = (P("dp", None), P("dp", "tensor"), P(None, "tensor"), P("dp", None, "tensor"))
    return jax.shard_map(
        functools.partial(on_device, nx, ny, nz),
        mesh=mesh,
        in_specs=placed,
        out_specs=(P(None, "tensor"), P("dp", None, "tensor")),
        check_vma=False,
    )
```

```python
import functools

import jax
import jax.numpy as jnp
from jax import lax
from jax.experimental import pallas as pl
from jax.experimental.pallas import tpu as pltpu
from jax.sharding import PartitionSpec as P

ridge_scale = 0.001
highest = lax.Precision.HIGHEST
f32 = jnp.float32
bf16 = jnp.bfloat16
MESH = pl.DeviceIdType.MESH
CORES = 2


def dot(a, b, ca, cb, precision=None):
    return lax.dot_general(
        a, b, (((ca,), (cb,)), ((), ())), precision=precision, preferred_element_type=f32
    )


def split(value):
    high = value.astype(bf16)
    return high, (value - high.astype(f32)).astype(bf16)


def dot3(a, b, ca, cb):
    return dot(a[0], b[0], ca, cb) + (dot(a[0], b[1], ca, cb) + dot(a[1], b[0], ca, cb))


def await_bytes(ref, sem):
    pltpu.make_async_copy(ref, ref, sem).wait()


def ring_order(n):
    return sorted(range(1, n), key=lambda k: -min(k, n - k))


def kernel(
    nx, ny, nz,
    act_hbm, grad_hbm, q_hbm, err_hbm, factor_ref, res_hbm,
    act, grads, q_prev, err, merged, part, from_core, half, xy_in, z_out, z_in, p_t,
    n_own, pair_in, cross_out, cross_in, n_all, table, res,
    load_sem, core_send, core_recv, xy_send, xy_recv, z_send, z_recv, ag_send, far_send, ag_recv,
    fw_send, fw_recv, pair_send, pair_recv, cross_send, cross_recv, back_send, back_recv, out_sem, known,
):
    rank, rows = p_t.shape
    nt = nx * ny
    hrank = rank // CORES
    crank = hrank // nx
    width = rows // ny
    quarter = rank // 4
    npair = nz // 2

    dp, t = lax.axis_index("dp"), lax.axis_index("tensor")
    z, c = lax.div(dp, CORES), lax.rem(dp, CORES)
    x, y = lax.div(t, ny), lax.rem(t, ny)

    def device(z_at, c_at, x_at, y_at):
        return {"dp": z_at * CORES + c_at, "tensor": x_at * ny + y_at}

    def around(at, step, n):
        return lax.rem(at + step, n)

    def send(src, dst, send_sem, recv_sem, to):
        pltpu.make_async_remote_copy(
            src_ref=src, dst_ref=dst, send_sem=send_sem, recv_sem=recv_sem,
            device_id=to, device_id_type=MESH,
        ).start()

    sibling = device(z, 1 - c, x, y)
    plane = sorted(
        ((dx, dy) for dx in range(nx) for dy in range(ny) if dx or dy),
        key=lambda d: -(min(d[0], nx - d[0]) + min(d[1], ny - d[1])),
    )
    ring = ring_order(nz)
    mate = z + 1 - 2 * lax.rem(z, 2)

    block_order = ring_order(ny) + [0]

    def columns(offset):
        return pl.ds(pl.multiple_of(around(y, offset, ny) * width, width), width)

    loads = [
        [pltpu.make_async_copy(grad_hbm, grads, load_sem.at[0]),
         pltpu.make_async_copy(q_hbm, q_prev, load_sem.at[1])]
    ]
    for k, offset in enumerate(block_order):
        at = columns(offset)
        loads.append([
            pltpu.make_async_copy(act_hbm.at[:, at], act.at[:, at], load_sem.at[2 + 2 * k]),
            pltpu.make_async_copy(err_hbm.at[0, at, :], err.at[at, :], load_sem.at[3 + 2 * k]),
        ])
    for group in loads:
        for copy in group:
            copy.start()

    barrier = pltpu.get_barrier_semaphore()
    near = [dz for dz in ring if min(dz, nz - dz) <= nz // 4]
    greeted = [device(z, c, around(x, dx, nx), around(y, dy, ny)) for dx, dy in plane]
    greeted += [device(around(z, dz, nz), c, x, y) for dz in near]
    greeted += [device(z, 1 - c, around(x, dx, nx), around(y, ny // 2, ny)) for dx in range(nx)]
    greeted += [device(mate, 1 - c, x, y), sibling]
    for other in greeted:
        pl.semaphore_signal(barrier, inc=1, device_id=other, device_id_type=MESH)

    own_half = pl.ds(pl.multiple_of(c * hrank, hrank), hrank)
    other_half = pl.ds(pl.multiple_of((1 - c) * hrank, hrank), hrank)

    def scatter(k, offset):
        at = columns(offset)
        await_bytes(from_core.at[k], core_recv.at[k])
        half[k] = part[own_half, at] + from_core[k]
        for dx in ring_order(nx) + [0]:
            to_x = around(x, dx, nx)
            mine = pl.ds(pl.multiple_of(to_x * crank, crank), crank)
            if dx == 0 and offset == 0:
                xy_in[t] = half[k, mine, :]
            else:
                send(half.at[k, mine, :], xy_in.at[t], xy_send, xy_recv,
                     device(z, c, to_x, around(y, offset, ny)))

    for copy in loads[0]:
        copy.wait()
    q_both = jnp.concatenate(split(q_prev[...]), axis=0)
    projected = dot(q_both, grads[...], 1, 1)
    projected = jnp.concatenate(split(projected[:rank] + projected[rank:]), axis=0)
    for k, offset in enumerate(block_order):
        at = columns(offset)
        for copy in loads[1 + k]:
            copy.wait()
        err_high, err_low = split(err[at, :])
        term = dot(projected, act[:, at], 1, 0) + dot(q_both, err_high, 1, 1)
        part[:, at] = (term[:rank] + term[rank:]) + dot(q_both[:rank], err_low, 1, 1)
        if k == 0:
            pl.semaphore_wait(barrier, len(greeted))
            for dz in (nz // 4, nz - nz // 4):
                pl.semaphore_signal(
                    known, inc=1, device_id=device(around(z, dz, nz), c, x, y), device_id_type=MESH
                )
        send(part.at[other_half, at], from_core.at[k], core_send, core_recv.at[k], sibling)
        if k > 0:
            scatter(k - 1, block_order[k - 1])
    scatter(ny - 1, block_order[-1])

    await_bytes(xy_in.at[pl.ds(0, nt - 1)], xy_recv)
    piece = jnp.sum(xy_in[...], axis=0)
    z_out[...] = piece
    pl.semaphore_wait(known, 2)
    for dz in ring:
        send(z_out, z_in.at[z], z_send, z_recv, device(around(z, dz, nz), c, x, y))
    z_in[z] = piece

    def gradient(k, carry):
        at = pl.ds(pl.multiple_of(k * width, width), width)
        merged[at, :] = dot(act[:, at], grads[...], 0, 0) + err[at, :]
        return carry

    lax.fori_loop(0, ny, gradient, 0)
    await_bytes(z_in.at[pl.ds(0, nz - 1)], z_recv)
    my_rows = pl.ds(pl.multiple_of(c * hrank + x * crank, crank), crank)
    my_piece = p_t.at[my_rows, columns(0)]
    my_piece[...] = jnp.sum(z_in[...], axis=0)

    far = ny // 2
    for dx, dy in plane:
        send(my_piece, my_piece, ag_send, ag_recv.at[(ny - dy) % ny],
             device(z, c, around(x, dx, nx), around(y, dy, ny)))
        if dy == far:
            send(my_piece, my_piece, far_send, ag_recv.at[far],
                 device(z, 1 - c, around(x, dx, nx), around(y, far, ny)))
    near_first = list(reversed(block_order))
    for offset in near_first:
        if offset != far:
            count = (nx - 1 if offset == 0 else nx) * crank
            await_bytes(p_t.at[pl.ds(0, count), pl.ds(0, width)], ag_recv.at[offset])
            piece_ref = p_t.at[own_half, columns(offset)]
            send(piece_ref, piece_ref, fw_send, fw_recv.at[offset], sibling)
    total = None
    for offset in near_first:
        at = columns(offset)
        if offset == far:
            await_bytes(p_t.at[:, pl.ds(0, width)], ag_recv.at[far])
        else:
            await_bytes(p_t.at[pl.ds(0, hrank), pl.ds(0, width)], fw_recv.at[offset])
        term = dot3(split(p_t[:, at]), split(merged[at, :]), 1, 0)
        total = term if total is None else total + term
    n_own[...] = total

    place = lax.rem(z, 2) * CORES + c

    def rows_of(at):
        return pl.ds(pl.multiple_of(at * quarter, quarter), quarter)

    group = [(mate, 1 - c), (mate, c), (z, 1 - c)]
    for z_at, c_at in group:
        there = lax.rem(z_at, 2) * CORES + c_at
        send(n_own.at[rows_of(there), :], pair_in.at[place], pair_send, pair_recv,
             device(z_at, c_at, x, y))
    pair_in[place] = n_own[rows_of(place), :]

    gram = dot(p_t[...], p_t[...], 1, 1, highest)
    row_at = lax.broadcasted_iota(jnp.int32, (rank, rank), 0)
    col_at = lax.broadcasted_iota(jnp.int32, (rank, rank), 1)
    eye = jnp.where(row_at == col_at, 1.0, 0.0).astype(f32)
    trace = jnp.sum(jnp.sum(gram * eye, axis=1, keepdims=True), axis=0, keepdims=True)
    shift = ridge_scale * rows * (trace / (rows * rank) + 1e-05)
    table[...] = jnp.concatenate([gram + shift * eye, eye], axis=1)
    rank_at = lax.broadcasted_iota(jnp.int32, (rank, 1), 0)

    def eliminate(first, last):
        def step(k, held):
            for j in range(8):
                row = held[j : j + 1, :]
                scale = held[:, j : j + 1] * (1.0 / row[:, j : j + 1])
                held = held - jnp.where((rank_at > j) & (rank_at < rank - 8 * k), scale, 0.0) * row
            held = jnp.concatenate([held[8:], held[:8]], axis=0)
            return pltpu.roll(held, 2 * rank - 8, 1)

        table[...] = lax.fori_loop(first, last, step, table[...])

    early = rank // 32
    eliminate(0, early)

    await_bytes(pair_in.at[pl.ds(0, 3)], pair_recv)
    piece = jnp.sum(pair_in[...], axis=0)
    cross_out[...] = piece
    pair_at = lax.div(z, 2)
    for dz in ring:
        if dz % 2 == 0:
            send(cross_out, cross_in.at[pair_at], cross_send, cross_recv,
                 device(around(z, dz, nz), c, x, y))
    cross_in[pair_at] = piece

    eliminate(early, rank // 8)
    pivots = jnp.sum(table[:, rank:] * eye, axis=1, keepdims=True)
    inverse = table[:, :rank] * (1.0 / jnp.sqrt(pivots))

    await_bytes(cross_in.at[pl.ds(0, npair - 1)], cross_recv)
    mine = n_all.at[rows_of(place), :]
    mine[...] = jnp.sum(cross_in[...], axis=0)
    for z_at, c_at in group:
        send(mine, mine, back_send, back_recv, device(z_at, c_at, x, y))
    await_bytes(n_all.at[pl.ds(0, 3 * quarter), :], back_recv)

    factor = dot(inverse, n_all[...], 1, 0, highest) * (1.0 / (nz * CORES))
    factor_ref[...] = factor
    back = split(dot(inverse, factor, 0, 0, highest))
    outs = []
    for offset in near_first:
        at = columns(offset)
        res[at, :] = merged[at, :] - dot3(split(p_t[:, at].T), back, 1, 0)
        outs.append(pltpu.make_async_copy(res.at[at, :], res_hbm.at[0, at, :], out_sem.at[offset]))
        outs[-1].start()

    await_bytes(from_core, core_send)
    await_bytes(xy_in.at[pl.ds(0, nt - 1)], xy_send)
    await_bytes(z_in.at[pl.ds(0, nz - 1)], z_send)
    await_bytes(xy_in.at[pl.ds(0, nt - 1)], ag_send)
    await_bytes(xy_in.at[pl.ds(0, nx)], far_send)
    await_bytes(from_core.at[pl.ds(0, ny - 1)], fw_send)
    await_bytes(pair_in.at[pl.ds(0, 3)], pair_send)
    await_bytes(cross_in.at[pl.ds(0, npair - 1)], cross_send)
    await_bytes(pair_in.at[pl.ds(0, 3)], back_send)
    for copy in outs:
        copy.wait()


def on_device(nx, ny, nz, activations, out_grads, q_previous, carried_error):
    tokens, rows = activations.shape
    width = out_grads.shape[1]
    rank = q_previous.shape[0]
    nt = nx * ny
    piece = (rank // CORES // nx, rows // ny)
    quarter = (rank // 4, width)
    vmem, dma = pltpu.VMEM, pltpu.SemaphoreType.DMA
    anywhere = pl.BlockSpec(memory_space=pl.ANY)
    factor, residual = pl.pallas_call(
        functools.partial(kernel, nx, ny, nz),
        name="powersgd",
        out_shape=(
            jax.ShapeDtypeStruct((rank, width), f32),
            jax.ShapeDtypeStruct((1, rows, width), f32),
        ),
        in_specs=[anywhere] * 4,
        out_specs=(pl.BlockSpec(memory_space=pltpu.VMEM), anywhere),
        scratch_shapes=[
            vmem((tokens, rows), bf16),
            vmem((tokens, width), bf16),
            vmem((rank, width), f32),
            vmem((rows, width), f32),
            vmem((rows, width), f32),
            vmem((rank, rows), f32),
            vmem((ny, rank // CORES, rows // ny), f32),
            vmem((ny, rank // CORES, rows // ny), f32),
            vmem((nt, *piece), f32),
            vmem(piece, f32),
            vmem((nz, *piece), f32),
            vmem((rank, rows), f32),
            vmem((rank, width), f32),
            vmem((4, *quarter), f32),
            vmem(quarter, f32),
            vmem((nz // 2, *quarter), f32),
            vmem((rank, width), f32),
            vmem((rank, 2 * rank), f32),
            vmem((rows, width), f32),
            dma((2 + 2 * ny,)),
            dma, dma((ny,)),
            dma, dma,
            dma, dma,
            dma, dma, dma((ny,)),
            dma, dma((ny,)),
            dma, dma,
            dma, dma,
            dma, dma,
            dma((ny,)),
            pltpu.SemaphoreType.REGULAR,
        ],
        compiler_params=pltpu.CompilerParams(
            collective_id=0, has_side_effects=True
        ),
    )(activations, out_grads, q_previous, carried_error)
    return factor, residual


def solution(mesh):
    nz = mesh.shape["dp"] // CORES
    nx = ny = {16: 4, 4: 2}[mesh.shape["tensor"]]
    placed = (P("dp", None), P("dp", "tensor"), P(None, "tensor"), P("dp", None, "tensor"))
    return jax.shard_map(
        functools.partial(on_device, nx, ny, nz),
        mesh=mesh,
        in_specs=placed,
        out_specs=(P(None, "tensor"), P("dp", None, "tensor")),
        check_vma=False,
    )
```

```python
import functools

import jax
import jax.numpy as jnp
from jax import lax
from jax.experimental import pallas as pl
from jax.experimental.pallas import tpu as pltpu
from jax.sharding import PartitionSpec as P

ridge_scale = 0.001
highest = lax.Precision.HIGHEST
f32 = jnp.float32
bf16 = jnp.bfloat16
MESH = pl.DeviceIdType.MESH
CORES = 2


def dot(a, b, ca, cb, precision=None):
    return lax.dot_general(
        a, b, (((ca,), (cb,)), ((), ())), precision=precision, preferred_element_type=f32
    )


def split(value):
    high = value.astype(bf16)
    return high, (value - high.astype(f32)).astype(bf16)


def dot3(a, b, ca, cb):
    return dot(a[0], b[0], ca, cb) + (dot(a[0], b[1], ca, cb) + dot(a[1], b[0], ca, cb))


def await_bytes(ref, sem):
    pltpu.make_async_copy(ref, ref, sem).wait()


def ring_order(n):
    return sorted(range(1, n), key=lambda k: -min(k, n - k))


def kernel(
    nx, ny, nz,
    act_hbm, grad_hbm, q_hbm, err_hbm, merged, p_t, n_all, inverse,
    act, grads, q_prev, err, part, from_core, half, xy_in, z_out, z_in,
    n_own, pair_in, cross_out, cross_in, table,
    load_sem, core_send, core_recv, xy_send, xy_recv, z_send, z_recv, ag_send, far_send, ag_recv,
    fw_send, fw_recv, pair_send, pair_recv, cross_send, cross_recv, back_send, back_recv, known,
):
    rank, rows = p_t.shape
    nt = nx * ny
    hrank = rank // CORES
    crank = hrank // nx
    width = rows // ny
    quarter = rank // 4
    npair = nz // 2

    dp, t = lax.axis_index("dp"), lax.axis_index("tensor")
    z, c = lax.div(dp, CORES), lax.rem(dp, CORES)
    x, y = lax.div(t, ny), lax.rem(t, ny)

    def device(z_at, c_at, x_at, y_at):
        return {"dp": z_at * CORES + c_at, "tensor": x_at * ny + y_at}

    def around(at, step, n):
        return lax.rem(at + step, n)

    def send(src, dst, send_sem, recv_sem, to):
        pltpu.make_async_remote_copy(
            src_ref=src, dst_ref=dst, send_sem=send_sem, recv_sem=recv_sem,
            device_id=to, device_id_type=MESH,
        ).start()

    sibling = device(z, 1 - c, x, y)
    plane = sorted(
        ((dx, dy) for dx in range(nx) for dy in range(ny) if dx or dy),
        key=lambda d: -(min(d[0], nx - d[0]) + min(d[1], ny - d[1])),
    )
    ring = ring_order(nz)
    mate = z + 1 - 2 * lax.rem(z, 2)

    block_order = ring_order(ny) + [0]

    def columns(offset):
        return pl.ds(pl.multiple_of(around(y, offset, ny) * width, width), width)

    loads = [
        [pltpu.make_async_copy(grad_hbm, grads, load_sem.at[0]),
         pltpu.make_async_copy(q_hbm, q_prev, load_sem.at[1])]
    ]
    for k, offset in enumerate(block_order):
        at = columns(offset)
        loads.append([
            pltpu.make_async_copy(act_hbm.at[:, at], act.at[:, at], load_sem.at[2 + 2 * k]),
            pltpu.make_async_copy(err_hbm.at[0, at, :], err.at[at, :], load_sem.at[3 + 2 * k]),
        ])
    for group in loads:
        for copy in group:
            copy.start()

    barrier = pltpu.get_barrier_semaphore()
    near = [dz for dz in ring if min(dz, nz - dz) <= nz // 4]
    greeted = [device(z, c, around(x, dx, nx), around(y, dy, ny)) for dx, dy in plane]
    greeted += [device(around(z, dz, nz), c, x, y) for dz in near]
    greeted += [device(z, 1 - c, around(x, dx, nx), around(y, ny // 2, ny)) for dx in range(nx)]
    greeted += [device(mate, 1 - c, x, y), sibling]
    for other in greeted:
        pl.semaphore_signal(barrier, inc=1, device_id=other, device_id_type=MESH)

    own_half = pl.ds(pl.multiple_of(c * hrank, hrank), hrank)
    other_half = pl.ds(pl.multiple_of((1 - c) * hrank, hrank), hrank)

    def scatter(k, offset):
        at = columns(offset)
        await_bytes(from_core.at[k], core_recv.at[k])
        half[k] = part[own_half, at] + from_core[k]
        for dx in ring_order(nx) + [0]:
            to_x = around(x, dx, nx)
            mine = pl.ds(pl.multiple_of(to_x * crank, crank), crank)
            if dx == 0 and offset == 0:
                xy_in[t] = half[k, mine, :]
            else:
                send(half.at[k, mine, :], xy_in.at[t], xy_send, xy_recv,
                     device(z, c, to_x, around(y, offset, ny)))

    for copy in loads[0]:
        copy.wait()
    q_both = jnp.concatenate(split(q_prev[...]), axis=0)
    projected = dot(q_both, grads[...], 1, 1)
    projected = jnp.concatenate(split(projected[:rank] + projected[rank:]), axis=0)
    for k, offset in enumerate(block_order):
        at = columns(offset)
        for copy in loads[1 + k]:
            copy.wait()
        err_high, err_low = split(err[at, :])
        term = dot(projected, act[:, at], 1, 0) + dot(q_both, err_high, 1, 1)
        part[:, at] = (term[:rank] + term[rank:]) + dot(q_both[:rank], err_low, 1, 1)
        if k == 0:
            pl.semaphore_wait(barrier, len(greeted))
            for dz in (nz // 4, nz - nz // 4):
                pl.semaphore_signal(
                    known, inc=1, device_id=device(around(z, dz, nz), c, x, y), device_id_type=MESH
                )
        send(part.at[other_half, at], from_core.at[k], core_send, core_recv.at[k], sibling)
        if k > 0:
            scatter(k - 1, block_order[k - 1])
    scatter(ny - 1, block_order[-1])

    await_bytes(xy_in.at[pl.ds(0, nt - 1)], xy_recv)
    piece = jnp.sum(xy_in[...], axis=0)
    z_out[...] = piece
    pl.semaphore_wait(known, 2)
    for dz in ring:
        send(z_out, z_in.at[z], z_send, z_recv, device(around(z, dz, nz), c, x, y))
    z_in[z] = piece

    def gradient(k, carry):
        at = pl.ds(pl.multiple_of(k * width, width), width)
        merged[at, :] = dot(act[:, at], grads[...], 0, 0) + err[at, :]
        return carry

    lax.fori_loop(0, ny, gradient, 0)
    await_bytes(z_in.at[pl.ds(0, nz - 1)], z_recv)
    my_rows = pl.ds(pl.multiple_of(c * hrank + x * crank, crank), crank)
    my_piece = p_t.at[my_rows, columns(0)]
    my_piece[...] = jnp.sum(z_in[...], axis=0)

    far = ny // 2
    for dx, dy in plane:
        send(my_piece, my_piece, ag_send, ag_recv.at[(ny - dy) % ny],
             device(z, c, around(x, dx, nx), around(y, dy, ny)))
        if dy == far:
            send(my_piece, my_piece, far_send, ag_recv.at[far],
                 device(z, 1 - c, around(x, dx, nx), around(y, far, ny)))
    near_first = list(reversed(block_order))
    for offset in near_first:
        if offset != far:
            count = (nx - 1 if offset == 0 else nx) * crank
            await_bytes(p_t.at[pl.ds(0, count), pl.ds(0, width)], ag_recv.at[offset])
            piece_ref = p_t.at[own_half, columns(offset)]
            send(piece_ref, piece_ref, fw_send, fw_recv.at[offset], sibling)
    total = None
    for offset in near_first:
        at = columns(offset)
        if offset == far:
            await_bytes(p_t.at[:, pl.ds(0, width)], ag_recv.at[far])
        else:
            await_bytes(p_t.at[pl.ds(0, hrank), pl.ds(0, width)], fw_recv.at[offset])
        term = dot3(split(p_t[:, at]), split(merged[at, :]), 1, 0)
        total = term if total is None else total + term
    n_own[...] = total

    place = lax.rem(z, 2) * CORES + c

    def rows_of(at):
        return pl.ds(pl.multiple_of(at * quarter, quarter), quarter)

    group = [(mate, 1 - c), (mate, c), (z, 1 - c)]
    for z_at, c_at in group:
        there = lax.rem(z_at, 2) * CORES + c_at
        send(n_own.at[rows_of(there), :], pair_in.at[place], pair_send, pair_recv,
             device(z_at, c_at, x, y))
    pair_in[place] = n_own[rows_of(place), :]

    gram = dot(p_t[...], p_t[...], 1, 1, highest)
    row_at = lax.broadcasted_iota(jnp.int32, (rank, rank), 0)
    col_at = lax.broadcasted_iota(jnp.int32, (rank, rank), 1)
    eye = jnp.where(row_at == col_at, 1.0, 0.0).astype(f32)
    trace = jnp.sum(jnp.sum(gram * eye, axis=1, keepdims=True), axis=0, keepdims=True)
    shift = ridge_scale * rows * (trace / (rows * rank) + 1e-05)
    table[...] = jnp.concatenate([gram + shift * eye, eye], axis=1)
    rank_at = lax.broadcasted_iota(jnp.int32, (rank, 1), 0)

    def eliminate(first, last):
        def step(k, held):
            for j in range(8):
                row = held[j : j + 1, :]
                scale = held[:, j : j + 1] * (1.0 / row[:, j : j + 1])
                held = held - jnp.where((rank_at > j) & (rank_at < rank - 8 * k), scale, 0.0) * row
            held = jnp.concatenate([held[8:], held[:8]], axis=0)
            return pltpu.roll(held, 2 * rank - 8, 1)

        table[...] = lax.fori_loop(first, last, step, table[...])

    early = rank // 32
    eliminate(0, early)

    await_bytes(pair_in.at[pl.ds(0, 3)], pair_recv)
    piece = jnp.sum(pair_in[...], axis=0)
    cross_out[...] = piece
    pair_at = lax.div(z, 2)
    for dz in ring:
        if dz % 2 == 0:
            send(cross_out, cross_in.at[pair_at], cross_send, cross_recv,
                 device(around(z, dz, nz), c, x, y))
    cross_in[pair_at] = piece

    eliminate(early, rank // 8)
    pivots = jnp.sum(table[:, rank:] * eye, axis=1, keepdims=True)
    inverse[...] = table[:, :rank] * (1.0 / jnp.sqrt(pivots))

    await_bytes(cross_in.at[pl.ds(0, npair - 1)], cross_recv)
    mine = n_all.at[rows_of(place), :]
    mine[...] = jnp.sum(cross_in[...], axis=0)
    for z_at, c_at in group:
        send(mine, mine, back_send, back_recv, device(z_at, c_at, x, y))
    await_bytes(n_all.at[pl.ds(0, 3 * quarter), :], back_recv)

    await_bytes(from_core, core_send)
    await_bytes(xy_in.at[pl.ds(0, nt - 1)], xy_send)
    await_bytes(z_in.at[pl.ds(0, nz - 1)], z_send)
    await_bytes(xy_in.at[pl.ds(0, nt - 1)], ag_send)
    await_bytes(xy_in.at[pl.ds(0, nx)], far_send)
    await_bytes(from_core.at[pl.ds(0, ny - 1)], fw_send)
    await_bytes(pair_in.at[pl.ds(0, 3)], pair_send)
    await_bytes(cross_in.at[pl.ds(0, npair - 1)], cross_send)
    await_bytes(pair_in.at[pl.ds(0, 3)], back_send)


def finish(replicas, merged, p_t, n_all, inverse, factor_hbm, res_hbm, factor, res, sems):
    rows = merged.shape[0]
    factor[...] = dot(inverse[...], n_all[...], 1, 0, highest) * (1.0 / replicas)
    out = pltpu.make_async_copy(factor, factor_hbm, sems.at[0])
    out.start()
    outs = [out]
    back = split(dot(inverse[...], factor[...], 0, 0, highest))
    step = rows // 4
    for k in range(4):
        at = pl.ds(k * step, step)
        res[at, :] = merged[at, :] - dot3(split(p_t[:, at].T), back, 1, 0)
        outs.append(pltpu.make_async_copy(res.at[at, :], res_hbm.at[0, at, :], sems.at[1 + k]))
        outs[-1].start()
    for out in outs:
        out.wait()


def on_device(nx, ny, nz, activations, out_grads, q_previous, carried_error):
    tokens, rows = activations.shape
    width = out_grads.shape[1]
    rank = q_previous.shape[0]
    nt = nx * ny
    piece = (rank // CORES // nx, rows // ny)
    quarter = (rank // 4, width)
    vmem, dma = pltpu.VMEM, pltpu.SemaphoreType.DMA
    anywhere = pl.BlockSpec(memory_space=pl.ANY)
    in_hbm = [
        pltpu.with_memory_space_constraint(a, pltpu.HBM)
        for a in (activations, out_grads, q_previous, carried_error)
    ]
    local = pl.BlockSpec(memory_space=pltpu.VMEM)
    passed = pl.pallas_call(
        functools.partial(kernel, nx, ny, nz),
        name="powersgd",
        out_shape=(
            vmem((rows, width), f32),
            vmem((rank, rows), f32),
            vmem((rank, width), f32),
            vmem((rank, rank), f32),
        ),
        in_specs=[anywhere] * 4,
        out_specs=(local,) * 4,
        scratch_shapes=[
            vmem((tokens, rows), bf16),
            vmem((tokens, width), bf16),
            vmem((rank, width), f32),
            vmem((rows, width), f32),
            vmem((rank, rows), f32),
            vmem((ny, rank // CORES, rows // ny), f32),
            vmem((ny, rank // CORES, rows // ny), f32),
            vmem((nt, *piece), f32),
            vmem(piece, f32),
            vmem((nz, *piece), f32),
            vmem((rank, width), f32),
            vmem((4, *quarter), f32),
            vmem(quarter, f32),
            vmem((nz // 2, *quarter), f32),
            vmem((rank, 2 * rank), f32),
            dma((2 + 2 * ny,)),
            dma, dma((ny,)),
            dma, dma,
            dma, dma,
            dma, dma, dma((ny,)),
            dma, dma((ny,)),
            dma, dma,
            dma, dma,
            dma, dma,
            pltpu.SemaphoreType.REGULAR,
        ],
        compiler_params=pltpu.CompilerParams(
            collective_id=0, has_side_effects=True, vmem_limit_bytes=16 * 1024 * 1024
        ),
    )(*in_hbm)
    return pl.pallas_call(
        functools.partial(finish, nz * CORES),
        name="residual",
        out_shape=(
            jax.ShapeDtypeStruct((rank, width), f32),
            jax.ShapeDtypeStruct((1, rows, width), f32),
        ),
        in_specs=[local] * 4,
        out_specs=(anywhere,) * 2,
        scratch_shapes=[vmem((rank, width), f32), vmem((rows, width), f32), dma((5,))],
        compiler_params=pltpu.CompilerParams(vmem_limit_bytes=16 * 1024 * 1024),
    )(*(pltpu.with_memory_space_constraint(a, pltpu.VMEM) for a in passed))


def solution(mesh):
    nz = mesh.shape["dp"] // CORES
    nx = ny = {16: 4, 4: 2}[mesh.shape["tensor"]]
    placed = (P("dp", None), P("dp", "tensor"), P(None, "tensor"), P("dp", None, "tensor"))
    return jax.shard_map(
        functools.partial(on_device, nx, ny, nz),
        mesh=mesh,
        in_specs=placed,
        out_specs=(P(None, "tensor"), P("dp", None, "tensor")),
        check_vma=False,
    )
```

```python
import functools

import jax
import jax.numpy as jnp
from jax import lax
from jax.experimental import pallas as pl
from jax.experimental.pallas import tpu as pltpu
from jax.sharding import PartitionSpec as P

ridge_scale = 0.001
highest = lax.Precision.HIGHEST
f32 = jnp.float32
bf16 = jnp.bfloat16
MESH = pl.DeviceIdType.MESH
CORES = 2


def dot(a, b, ca, cb, precision=None):
    return lax.dot_general(
        a, b, (((ca,), (cb,)), ((), ())), precision=precision, preferred_element_type=f32
    )


def split(value):
    high = value.astype(bf16)
    return high, (value - high.astype(f32)).astype(bf16)


def dot3(a, b, ca, cb):
    return dot(a[0], b[0], ca, cb) + (dot(a[0], b[1], ca, cb) + dot(a[1], b[0], ca, cb))


def await_bytes(ref, sem):
    pltpu.make_async_copy(ref, ref, sem).wait()


def ring_order(n):
    return sorted(range(1, n), key=lambda k: -min(k, n - k))


def kernel(
    nx, ny, nz,
    act_hbm, grad_hbm, q_hbm, err_hbm, merged, basis, n_all, inverse,
    act, grads, q_prev, err, part, from_core, half, xy_in, z_out, z_in, p_t,
    packed, m_core, m_out, m_own, m_mate, m_high, m_low, cross_out, cross_in, table,
    load_sem, core_send, core_recv, xy_send, xy_recv, z_send, z_recv, ag_send, ag_recv,
    fw_send, fw_recv, pack_send, pack_recv, mate_send, mate_recv,
    cross_send, cross_recv, back_send, back_recv, known,
):
    rank, rows = p_t.shape
    width = merged.shape[1]
    nt = nx * ny
    half_rows = rows // CORES
    block = half_rows // 2
    prank, pcols = rank // nx, half_rows // ny
    npair = nz // 2
    ncol = width // 4

    dp, t = lax.axis_index("dp"), lax.axis_index("tensor")
    z, c = lax.div(dp, CORES), lax.rem(dp, CORES)
    x, y = lax.div(t, ny), lax.rem(t, ny)
    odd = lax.rem(z, 2)
    mate = z + 1 - 2 * odd

    def device(z_at, c_at, x_at, y_at):
        return {"dp": z_at * CORES + c_at, "tensor": x_at * ny + y_at}

    def around(at, step, n):
        return lax.rem(at + step, n)

    def span(start, size):
        return pl.ds(pl.multiple_of(start, size), size)

    def send(src, dst, send_sem, recv_sem, to):
        pltpu.make_async_remote_copy(
            src_ref=src, dst_ref=dst, send_sem=send_sem, recv_sem=recv_sem,
            device_id=to, device_id_type=MESH,
        ).start()

    sibling = device(z, 1 - c, x, y)
    plane = sorted(
        ((dx, dy) for dx in range(nx) for dy in range(ny) if dx or dy),
        key=lambda d: -(min(d[0], nx - d[0]) + min(d[1], ny - d[1])),
    )
    ring = ring_order(nz)

    loads = [
        [pltpu.make_async_copy(grad_hbm, grads, load_sem.at[0]),
         pltpu.make_async_copy(q_hbm, q_prev, load_sem.at[1])]
    ]
    starts = [h * half_rows + j * block for h in (1 - c, c) for j in range(2)]
    for k, start in enumerate(starts):
        at = span(start, block)
        loads.append([
            pltpu.make_async_copy(act_hbm.at[:, at], act.at[:, at], load_sem.at[2 + 2 * k]),
            pltpu.make_async_copy(err_hbm.at[0, at, :], err.at[at, :], load_sem.at[3 + 2 * k]),
        ])
    for group in loads:
        for copy in group:
            copy.start()

    barrier = pltpu.get_barrier_semaphore()
    near = [dz for dz in ring if min(dz, nz - dz) <= nz // 4]
    greeted = [device(z, c, around(x, dx, nx), around(y, dy, ny)) for dx, dy in plane]
    greeted += [device(around(z, dz, nz), c, x, y) for dz in near]
    greeted += [device(mate, 1 - c, x, y), sibling]
    for other in greeted:
        pl.semaphore_signal(barrier, inc=1, device_id=other, device_id_type=MESH)

    for copy in loads[0]:
        copy.wait()
    q_both = jnp.concatenate(split(q_prev[...]), axis=0)
    projected = dot(q_both, grads[...], 1, 1)
    projected = jnp.concatenate(split(projected[:rank] + projected[rank:]), axis=0)
    for k, start in enumerate(starts):
        at = span(start, block)
        for copy in loads[1 + k]:
            copy.wait()
        err_high, err_low = split(err[at, :])
        term = dot(projected, act[:, at], 1, 0) + dot(q_both, err_high, 1, 1)
        part[:, at] = (term[:rank] + term[rank:]) + dot(q_both[:rank], err_low, 1, 1)
        if k == 1:
            pl.semaphore_wait(barrier, len(greeted))
            send(part.at[:, span((1 - c) * half_rows, half_rows)], from_core,
                 core_send, core_recv, sibling)
            for dz in (nz // 4, nz - nz // 4):
                pl.semaphore_signal(
                    known, inc=1, device_id=device(around(z, dz, nz), c, x, y), device_id_type=MESH
                )

    own_half = span(c * half_rows, half_rows)
    await_bytes(from_core, core_recv)
    half[...] = part[:, own_half] + from_core[...]

    def piece_of(ref, x_at, y_at):
        return ref.at[span(x_at * prank, prank), span(y_at * pcols, pcols)]

    for dx, dy in plane:
        x_at, y_at = around(x, dx, nx), around(y, dy, ny)
        send(piece_of(half, x_at, y_at), xy_in.at[t], xy_send, xy_recv, device(z, c, x_at, y_at))
    xy_in[t] = piece_of(half, x, y)[...]

    def gradient(k, carry):
        top_at, low_at = span(k * block, block), span(half_rows + k * block, block)
        top = dot(act[:, top_at], grads[...], 0, 0) + err[top_at, :]
        low = dot(act[:, low_at], grads[...], 0, 0) + err[low_at, :]
        merged[top_at, :] = top
        merged[low_at, :] = low
        for core in range(CORES):
            for parity in range(2):
                at = (parity * CORES + core) * ncol
                packed[core, parity, top_at, :] = jnp.concatenate(
                    [top[:, at : at + ncol], low[:, at : at + ncol]], axis=1
                )
        return carry

    lax.fori_loop(0, 2, gradient, 0)
    send(packed.at[1 - c], m_core, pack_send, pack_recv, sibling)

    await_bytes(xy_in.at[pl.ds(0, nt - 1)], xy_recv)
    piece = jnp.sum(xy_in[...], axis=0)
    z_out[...] = piece
    pl.semaphore_wait(known, 2)
    for dz in ring:
        send(z_out, z_in.at[z], z_send, z_recv, device(around(z, dz, nz), c, x, y))
    z_in[z] = piece

    await_bytes(m_core, pack_recv)
    m_out[...] = packed[c, 1 - odd] + m_core[1 - odd]
    send(m_out, m_mate, mate_send, mate_recv, device(mate, c, x, y))
    m_own[...] = packed[c, odd] + m_core[odd]

    await_bytes(z_in.at[pl.ds(0, nz - 1)], z_recv)

    def mine_of(x_at, y_at):
        return p_t.at[span(x_at * prank, prank), span(c * half_rows + y_at * pcols, pcols)]

    my_piece = mine_of(x, y)
    my_piece[...] = jnp.sum(z_in[...], axis=0)

    for dx, dy in plane:
        send(my_piece, my_piece, ag_send, ag_recv.at[(ny - dy) % ny],
             device(z, c, around(x, dx, nx), around(y, dy, ny)))
    await_bytes(m_mate, mate_recv)
    m_high[...], m_low[...] = split(m_own[...] + m_mate[...])
    near_first = [0] + list(reversed(ring_order(ny)))
    for offset in near_first:
        count = (nx - 1 if offset == 0 else nx) * prank
        await_bytes(p_t.at[pl.ds(0, count), pl.ds(0, pcols)], ag_recv.at[offset])
        ready = p_t.at[:, span(c * half_rows + around(y, offset, ny) * pcols, pcols)]
        send(ready, ready, fw_send, fw_recv.at[offset], sibling)

    total = jnp.zeros((2 * rank, 2 * ncol), f32)
    for offset in near_first:
        await_bytes(p_t.at[:, pl.ds(0, pcols)], fw_recv.at[offset])
        first = around(y, offset, ny) * pcols
        at = span(first, pcols)
        both = jnp.concatenate([p_t[:, at], p_t[:, span(half_rows + first, pcols)]], axis=0)
        total += dot3(split(both), (m_high[at, :], m_low[at, :]), 1, 0)
    terms = total[:rank, :ncol] + total[rank:, ncol:]
    terms = jnp.concatenate([terms[: rank // 2], terms[rank // 2 :]], axis=1)
    cross_out[...] = terms

    pair_at = lax.div(z, 2)
    for dz in ring:
        if dz % 2 == 0:
            send(cross_out, cross_in.at[pair_at], cross_send, cross_recv,
                 device(around(z, dz, nz), c, x, y))
    cross_in[pair_at] = terms

    gram = dot(p_t[...], p_t[...], 1, 1, highest)
    row_at = lax.broadcasted_iota(jnp.int32, (rank, rank), 0)
    col_at = lax.broadcasted_iota(jnp.int32, (rank, rank), 1)
    eye = jnp.where(row_at == col_at, 1.0, 0.0).astype(f32)
    trace = jnp.sum(jnp.sum(gram * eye, axis=1, keepdims=True), axis=0, keepdims=True)
    shift = ridge_scale * rows * (trace / (rows * rank) + 1e-05)
    table[...] = jnp.concatenate([gram + shift * eye, eye], axis=1)
    rank_at = lax.broadcasted_iota(jnp.int32, (rank, 1), 0)

    def eliminate(k, held):
        for j in range(8):
            row = held[j : j + 1, :]
            scale = held[:, j : j + 1] * (1.0 / row[:, j : j + 1])
            held = held - jnp.where((rank_at > j) & (rank_at < rank - 8 * k), scale, 0.0) * row
        held = jnp.concatenate([held[8:], held[:8]], axis=0)
        return pltpu.roll(held, 2 * rank - 8, 1)

    table[...] = lax.fori_loop(0, rank // 8, eliminate, table[...])

    await_bytes(cross_in.at[pl.ds(0, npair - 1)], cross_recv)
    place = odd * CORES + c
    n_all[place] = jnp.sum(cross_in[...], axis=0)
    for z_at, c_at in ((mate, 1 - c), (mate, c), (z, 1 - c)):
        send(n_all.at[place], n_all.at[place], back_send, back_recv, device(z_at, c_at, x, y))

    pivots = jnp.sum(table[:, rank:] * eye, axis=1, keepdims=True)
    inverse[...] = table[:, :rank] * (1.0 / jnp.sqrt(pivots))

    def transposed(k, carry):
        at = span(k * block, block)
        high, low = split(p_t[:, at].T)
        basis[at, :] = jnp.concatenate([high, low, high, jnp.zeros_like(high)], axis=1)
        return carry

    lax.fori_loop(0, rows // block, transposed, 0)

    await_bytes(n_all.at[pl.ds(0, 3)], back_recv)
    await_bytes(from_core, core_send)
    await_bytes(xy_in.at[pl.ds(0, nt - 1)], xy_send)
    await_bytes(m_core, pack_send)
    await_bytes(z_in.at[pl.ds(0, nz - 1)], z_send)
    await_bytes(m_mate, mate_send)
    await_bytes(xy_in.at[pl.ds(0, nt - 1)], ag_send)
    await_bytes(from_core, fw_send)
    await_bytes(cross_in.at[pl.ds(0, npair - 1)], cross_send)
    await_bytes(n_all.at[pl.ds(0, 3)], back_send)


def finish(replicas, merged, basis, n_all, inverse, factor_hbm, res_hbm, factor, res, sems):
    rows = merged.shape[0]
    ncol = n_all.shape[2] // 2
    top = jnp.concatenate([n_all[k][:, :ncol] for k in range(4)], axis=1)
    low = jnp.concatenate([n_all[k][:, ncol:] for k in range(4)], axis=1)
    terms = jnp.concatenate([top, low], axis=0)
    factor[...] = dot(inverse[...], terms, 1, 0, highest) * (1.0 / replicas)
    out = pltpu.make_async_copy(factor, factor_hbm, sems.at[0])
    out.start()
    outs = [out]
    high, low = split(dot(inverse[...], factor[...], 0, 0, highest))
    back = jnp.concatenate([high, high, low, jnp.zeros_like(low)], axis=0)
    step = rows // 4
    for k in range(4):
        at = pl.ds(k * step, step)
        res[at, :] = merged[at, :] - dot(basis[at, :], back, 1, 0)
        outs.append(pltpu.make_async_copy(res.at[at, :], res_hbm.at[0, at, :], sems.at[1 + k]))
        outs[-1].start()
    for out in outs:
        out.wait()


def on_device(nx, ny, nz, activations, out_grads, q_previous, carried_error):
    tokens, rows = activations.shape
    width = out_grads.shape[1]
    rank = q_previous.shape[0]
    half_rows = rows // CORES
    piece = (rank // nx, half_rows // ny)
    columns = (half_rows, width // 2)
    terms = (rank // 2, width // 2)
    vmem, dma = pltpu.VMEM, pltpu.SemaphoreType.DMA
    anywhere = pl.BlockSpec(memory_space=pl.ANY)
    local = pl.BlockSpec(memory_space=pltpu.VMEM)
    in_hbm = [
        pltpu.with_memory_space_constraint(a, pltpu.HBM)
        for a in (activations, out_grads, q_previous, carried_error)
    ]
    passed = pl.pallas_call(
        functools.partial(kernel, nx, ny, nz),
        name="powersgd",
        out_shape=(
            vmem((rows, width), f32),
            vmem((rows, 4 * rank), bf16),
            vmem((4, *terms), f32),
            vmem((rank, rank), f32),
        ),
        in_specs=[anywhere] * 4,
        out_specs=(local,) * 4,
        scratch_shapes=[
            vmem((tokens, rows), bf16),
            vmem((tokens, width), bf16),
            vmem((rank, width), f32),
            vmem((rows, width), f32),
            vmem((rank, rows), f32),
            vmem((rank, half_rows), f32),
            vmem((rank, half_rows), f32),
            vmem((nx * ny, *piece), f32),
            vmem(piece, f32),
            vmem((nz, *piece), f32),
            vmem((rank, rows), f32),
            vmem((CORES, 2, *columns), f32),
            vmem((2, *columns), f32),
            vmem(columns, f32),
            vmem(columns, f32),
            vmem(columns, f32),
            vmem(columns, bf16),
            vmem(columns, bf16),
            vmem(terms, f32),
            vmem((nz // 2, *terms), f32),
            vmem((rank, 2 * rank), f32),
            dma((10,)),
            dma, dma,
            dma, dma,
            dma, dma,
            dma, dma((ny,)),
            dma, dma((ny,)),
            dma, dma,
            dma, dma,
            dma, dma,
            dma, dma,
            pltpu.SemaphoreType.REGULAR,
        ],
        compiler_params=pltpu.CompilerParams(
            collective_id=0, has_side_effects=True, vmem_limit_bytes=20 * 1024 * 1024
        ),
    )(*in_hbm)
    return pl.pallas_call(
        functools.partial(finish, nz * CORES),
        name="residual",
        out_shape=(
            jax.ShapeDtypeStruct((rank, width), f32),
            jax.ShapeDtypeStruct((1, rows, width), f32),
        ),
        in_specs=[local] * 4,
        out_specs=(anywhere,) * 2,
        scratch_shapes=[vmem((rank, width), f32), vmem((rows, width), f32), dma((5,))],
        compiler_params=pltpu.CompilerParams(vmem_limit_bytes=16 * 1024 * 1024),
    )(*(pltpu.with_memory_space_constraint(a, pltpu.VMEM) for a in passed))


def solution(mesh):
    nz = mesh.shape["dp"] // CORES
    nx = ny = {16: 4, 4: 2}[mesh.shape["tensor"]]
    placed = (P("dp", None), P("dp", "tensor"), P(None, "tensor"), P("dp", None, "tensor"))
    return jax.shard_map(
        functools.partial(on_device, nx, ny, nz),
        mesh=mesh,
        in_specs=placed,
        out_specs=(P(None, "tensor"), P("dp", None, "tensor")),
        check_vma=False,
    )
```

```python
import functools

import jax
import jax.numpy as jnp
from jax import lax
from jax.experimental import pallas as pl
from jax.experimental.pallas import tpu as pltpu
from jax.sharding import PartitionSpec as P

ridge_scale = 0.001
highest = lax.Precision.HIGHEST
f32 = jnp.float32
bf16 = jnp.bfloat16
MESH = pl.DeviceIdType.MESH
CORES = 2
FAR = {4: 5, 2: 1}


def dot(a, b, ca, cb, precision=None):
    return lax.dot_general(
        a, b, (((ca,), (cb,)), ((), ())), precision=precision, preferred_element_type=f32
    )


def split(value):
    high = value.astype(bf16)
    return high, (value - high.astype(f32)).astype(bf16)


def dot3(a, b, ca, cb):
    return dot(a[0], b[0], ca, cb) + (dot(a[0], b[1], ca, cb) + dot(a[1], b[0], ca, cb))


def await_bytes(ref, sem):
    pltpu.make_async_copy(ref, ref, sem).wait()


def ring_order(n):
    return sorted(range(1, n), key=lambda k: -min(k, n - k))


def kernel(
    nx, ny, nz,
    act_hbm, grad_hbm, q_hbm, err_hbm, merged, basis, n_all, inverse,
    act, grads, q_prev, err, part, from_core, half, xy_in, z_out, z_in, p_t,
    m_core, m_out, m_mate, m_pair, cross_out, cross_in, table,
    load_sem, core_send, core_recv, xy_send, xy_recv, z_send, z_recv, ag_send, ag_recv,
    fw_send, fw_recv, m_send, m_recv, mate_send, mate_recv, pair_send, pair_recv,
    cross_send, cross_recv, back_send, back_recv, known,
):
    rank, rows = p_t.shape
    width = merged.shape[1]
    nt = nx * ny
    half_rows = rows // CORES
    half_rank = rank // CORES
    block = rows // 4
    prank, pcols = half_rank // nx, rows // ny
    npair = nz // 2
    half_width = width // 2

    dp, t = lax.axis_index("dp"), lax.axis_index("tensor")
    z, c = lax.div(dp, CORES), lax.rem(dp, CORES)
    x, y = lax.div(t, ny), lax.rem(t, ny)
    odd = lax.rem(z, 2)
    mate = z + 1 - 2 * odd

    def device(z_at, c_at, x_at, y_at):
        return {"dp": z_at * CORES + c_at, "tensor": x_at * ny + y_at}

    def around(at, step, n):
        return lax.rem(at + step, n)

    def span(start, size):
        return pl.ds(pl.multiple_of(start, size), size)

    def send(src, dst, send_sem, recv_sem, to):
        pltpu.make_async_remote_copy(
            src_ref=src, dst_ref=dst, send_sem=send_sem, recv_sem=recv_sem,
            device_id=to, device_id_type=MESH,
        ).start()

    sibling = device(z, 1 - c, x, y)
    plane = sorted(
        ((dx, dy) for dx in range(nx) for dy in range(ny) if dx or dy),
        key=lambda d: -(min(d[0], nx - d[0]) + min(d[1], ny - d[1])),
    )
    far = [d for d in plane if min(d[0], nx - d[0]) + min(d[1], ny - d[1]) > nx // 2]
    near_plane = [d for d in plane if d not in far]
    ring = ring_order(nz)

    loads = [
        [pltpu.make_async_copy(grad_hbm, grads, load_sem.at[0]),
         pltpu.make_async_copy(q_hbm, q_prev, load_sem.at[1])]
    ]
    for k in range(4):
        at = pl.ds(k * block, block)
        loads.append([
            pltpu.make_async_copy(act_hbm.at[:, at], act.at[:, at], load_sem.at[2 + 2 * k]),
            pltpu.make_async_copy(err_hbm.at[0, at, :], err.at[at, :], load_sem.at[3 + 2 * k]),
        ])
    barrier = pltpu.get_barrier_semaphore()
    near = [dz for dz in ring if min(dz, nz - dz) <= nz // 4]
    greeted = [
        (min(dx, nx - dx) + min(dy, ny - dy), device(z, c, around(x, dx, nx), around(y, dy, ny)))
        for dx, dy in plane
    ]
    greeted += [(min(dz, nz - dz), device(around(z, dz, nz), c, x, y)) for dz in near]
    greeted += [
        (min(dx, nx - dx) + min(dy, ny - dy), device(z, 1 - c, around(x, dx, nx), around(y, dy, ny)))
        for dx, dy in far
    ]
    greeted += [(1, device(mate, 1 - c, x, y)), (0, sibling)]
    for _, other in sorted(greeted, key=lambda pair: -pair[0]):
        pl.semaphore_signal(barrier, inc=1, device_id=other, device_id_type=MESH)
    for group in loads:
        for copy in group:
            copy.start()

    def gradient(k, carry):
        at = span(k * block, block)
        merged[at, :] = dot(act[:, at], grads[...], 0, 0) + err[at, :]
        return carry

    for copy in loads[0]:
        copy.wait()
    q_both = jnp.concatenate(split(q_prev[...]), axis=0)
    projected = dot(q_both, grads[...], 1, 1)
    projected = jnp.concatenate(split(projected[:rank] + projected[rank:]), axis=0)
    for k in range(4):
        at = pl.ds(k * block, block)
        for copy in loads[1 + k]:
            copy.wait()
        err_high, err_low = split(err[at, :])
        term = dot(projected, act[:, at], 1, 0) + dot(q_both, err_high, 1, 1)
        part[:, at] = (term[:rank] + term[rank:]) + dot(q_both[:rank], err_low, 1, 1)

    pl.semaphore_wait(barrier, len(greeted))

    own_ranks = span(c * half_rank, half_rank)
    for k, (dx, dy) in enumerate(far):
        x_at, y_at = around(x, dx, nx), around(y, dy, ny)
        for c_at, slot in ((c, 0), (1 - c, 1)):
            rows_at = span(c_at * half_rank + x_at * prank, prank)
            send(part.at[rows_at, span(y_at * pcols, pcols)], xy_in.at[2 * k + slot],
                 xy_send, xy_recv, device(z, c_at, x_at, y_at))
    send(part.at[span((1 - c) * half_rank, half_rank), :], from_core, core_send, core_recv, sibling)
    for dz in (nz // 4, nz - nz // 4):
        pl.semaphore_signal(
            known, inc=1, device_id=device(around(z, dz, nz), c, x, y), device_id_type=MESH
        )
    await_bytes(from_core, core_recv)
    half[...] = part[own_ranks, :] + from_core[...]

    def piece_of(ref, x_at, y_at):
        return ref.at[span(x_at * prank, prank), span(y_at * pcols, pcols)]

    for k, (dx, dy) in enumerate(near_plane):
        x_at, y_at = around(x, dx, nx), around(y, dy, ny)
        send(piece_of(half, x_at, y_at), xy_in.at[2 * len(far) + k],
             xy_send, xy_recv, device(z, c, x_at, y_at))
    arriving = nt - 1 + len(far)
    xy_in[arriving] = piece_of(half, x, y)[...]

    lax.fori_loop(0, 4, gradient, 0)
    own_rows = span(c * half_rows, half_rows)
    send(merged.at[span((1 - c) * half_rows, half_rows), :], m_core, m_send, m_recv, sibling)

    def to_mate():
        await_bytes(m_core, m_recv)
        there = span((1 - odd) * half_width, half_width)
        m_out[...] = merged[own_rows, there] + m_core[:, there]
        send(m_out, m_mate, mate_send, mate_recv, device(mate, c, x, y))
        here = span(odd * half_width, half_width)
        m_pair[own_rows, :] = merged[own_rows, here] + m_core[:, here]

    def to_sibling():
        await_bytes(m_mate, mate_recv)
        m_pair[own_rows, :] += m_mate[...]
        send(m_pair.at[own_rows, :], m_pair.at[own_rows, :], pair_send, pair_recv, sibling)

    await_bytes(xy_in.at[pl.ds(0, arriving)], xy_recv)
    piece = jnp.sum(xy_in[...], axis=0)
    z_out[...] = piece
    pl.semaphore_wait(known, 2)
    for dz in ring:
        send(z_out, z_in.at[z], z_send, z_recv, device(around(z, dz, nz), c, x, y))
    z_in[z] = piece

    to_mate()
    await_bytes(z_in.at[pl.ds(0, nz - 1)], z_recv)

    my_piece = p_t.at[span(c * half_rank + x * prank, prank), span(y * pcols, pcols)]
    my_piece[...] = jnp.sum(z_in[...], axis=0)

    for dx, dy in plane:
        send(my_piece, my_piece, ag_send, ag_recv.at[(ny - dy) % ny],
             device(z, c, around(x, dx, nx), around(y, dy, ny)))
    to_sibling()
    await_bytes(m_pair.at[pl.ds(0, half_rows), :], pair_recv)
    near_first = [0] + list(reversed(ring_order(ny)))
    terms = None
    for offset in near_first:
        count = (nx - 1 if offset == 0 else nx) * prank
        await_bytes(p_t.at[pl.ds(0, count), pl.ds(0, pcols)], ag_recv.at[offset])
        at = span(around(y, offset, ny) * pcols, pcols)
        ready = p_t.at[own_ranks, at]
        send(ready, ready, fw_send, fw_recv, sibling)
        term = dot3(split(ready[...]), split(m_pair[at, :]), 1, 0)
        terms = term if terms is None else terms + term
    cross_out[...] = terms

    pair_at = lax.div(z, 2)
    for dz in ring:
        if dz % 2 == 0:
            send(cross_out, cross_in.at[pair_at], cross_send, cross_recv,
                 device(around(z, dz, nz), c, x, y))
    cross_in[pair_at] = terms

    await_bytes(from_core, fw_recv)
    gram = dot(p_t[...], p_t[...], 1, 1, highest)
    row_at = lax.broadcasted_iota(jnp.int32, (rank, rank), 0)
    col_at = lax.broadcasted_iota(jnp.int32, (rank, rank), 1)
    eye = jnp.where(row_at == col_at, 1.0, 0.0).astype(f32)
    trace = jnp.sum(jnp.sum(gram * eye, axis=1, keepdims=True), axis=0, keepdims=True)
    shift = ridge_scale * rows * (trace / (rows * rank) + 1e-05)
    table[...] = jnp.concatenate([gram + shift * eye, eye], axis=1)
    rank_at = lax.broadcasted_iota(jnp.int32, (rank, 1), 0)

    def eliminate(k, held):
        for j in range(8):
            row = held[j : j + 1, :]
            scale = held[:, j : j + 1] * (1.0 / row[:, j : j + 1])
            held = held - jnp.where((rank_at > j) & (rank_at < rank - 8 * k), scale, 0.0) * row
        held = jnp.concatenate([held[8:], held[:8]], axis=0)
        return pltpu.roll(held, 2 * rank - 8, 1)

    table[...] = lax.fori_loop(0, rank // 8, eliminate, table[...])

    await_bytes(cross_in.at[pl.ds(0, npair - 1)], cross_recv)
    place = odd * CORES + c
    n_all[place] = jnp.sum(cross_in[...], axis=0)
    for z_at, c_at in ((mate, 1 - c), (mate, c), (z, 1 - c)):
        send(n_all.at[place], n_all.at[place], back_send, back_recv, device(z_at, c_at, x, y))

    pivots = jnp.sum(table[:, rank:] * eye, axis=1, keepdims=True)
    inverse[...] = table[:, :rank] * (1.0 / jnp.sqrt(pivots))

    def transposed(k, carry):
        at = span(k * block, block)
        high, low = split(p_t[:, at].T)
        basis[at, :] = jnp.concatenate([high, low, high, jnp.zeros_like(high)], axis=1)
        return carry

    lax.fori_loop(0, rows // block, transposed, 0)

    await_bytes(n_all.at[pl.ds(0, 3)], back_recv)
    await_bytes(from_core, core_send)
    await_bytes(xy_in.at[pl.ds(0, arriving)], xy_send)
    await_bytes(m_core, m_send)
    await_bytes(z_in.at[pl.ds(0, nz - 1)], z_send)
    await_bytes(m_mate, mate_send)
    await_bytes(m_pair.at[pl.ds(0, half_rows), :], pair_send)
    await_bytes(xy_in.at[pl.ds(0, nt - 1)], ag_send)
    await_bytes(from_core, fw_send)
    await_bytes(cross_in.at[pl.ds(0, npair - 1)], cross_send)
    await_bytes(n_all.at[pl.ds(0, 3)], back_send)


def finish(replicas, merged, basis, n_all, inverse, factor_hbm, res_hbm, factor, res, sems):
    rows = merged.shape[0]
    terms = jnp.concatenate([
        jnp.concatenate([n_all[k], n_all[CORES + k]], axis=1) for k in range(CORES)
    ], axis=0)
    factor[...] = dot(inverse[...], terms, 1, 0, highest) * (1.0 / replicas)
    out = pltpu.make_async_copy(factor, factor_hbm, sems.at[0])
    out.start()
    outs = [out]
    high, low = split(dot(inverse[...], factor[...], 0, 0, highest))
    back = jnp.concatenate([high, high, low, jnp.zeros_like(low)], axis=0)
    step = rows // 4
    for k in range(4):
        at = pl.ds(k * step, step)
        res[at, :] = merged[at, :] - dot(basis[at, :], back, 1, 0)
        outs.append(pltpu.make_async_copy(res.at[at, :], res_hbm.at[0, at, :], sems.at[1 + k]))
        outs[-1].start()
    for out in outs:
        out.wait()


def on_device(nx, ny, nz, activations, out_grads, q_previous, carried_error):
    tokens, rows = activations.shape
    width = out_grads.shape[1]
    rank = q_previous.shape[0]
    half_rows = rows // CORES
    half_rank, half_width = rank // CORES, width // 2
    piece = (half_rank // nx, rows // ny)
    columns = (half_rows, half_width)
    terms = (half_rank, half_width)
    vmem, dma = pltpu.VMEM, pltpu.SemaphoreType.DMA
    anywhere = pl.BlockSpec(memory_space=pl.ANY)
    local = pl.BlockSpec(memory_space=pltpu.VMEM)
    in_hbm = [
        pltpu.with_memory_space_constraint(a, pltpu.HBM)
        for a in (activations, out_grads, q_previous, carried_error)
    ]
    passed = pl.pallas_call(
        functools.partial(kernel, nx, ny, nz),
        name="powersgd",
        out_shape=(
            vmem((rows, width), f32),
            vmem((rows, 4 * rank), bf16),
            vmem((4, *terms), f32),
            vmem((rank, rank), f32),
        ),
        in_specs=[anywhere] * 4,
        out_specs=(local,) * 4,
        scratch_shapes=[
            vmem((tokens, rows), bf16),
            vmem((tokens, width), bf16),
            vmem((rank, width), f32),
            vmem((rows, width), f32),
            vmem((rank, rows), f32),
            vmem((half_rank, rows), f32),
            vmem((half_rank, rows), f32),
            vmem((nx * ny + FAR[nx], *piece), f32),
            vmem(piece, f32),
            vmem((nz, *piece), f32),
            vmem((rank, rows), f32),
            vmem((half_rows, width), f32),
            vmem(columns, f32),
            vmem(columns, f32),
            vmem((rows, half_width), f32),
            vmem(terms, f32),
            vmem((nz // 2, *terms), f32),
            vmem((rank, 2 * rank), f32),
            dma((10,)),
            dma, dma,
            dma, dma,
            dma, dma,
            dma, dma((ny,)),
            dma, dma,
            dma, dma,
            dma, dma,
            dma, dma,
            dma, dma,
            dma, dma,
            pltpu.SemaphoreType.REGULAR,
        ],
        compiler_params=pltpu.CompilerParams(
            collective_id=0, has_side_effects=True, vmem_limit_bytes=20 * 1024 * 1024
        ),
    )(*in_hbm)
    return pl.pallas_call(
        functools.partial(finish, nz * CORES),
        name="residual",
        out_shape=(
            jax.ShapeDtypeStruct((rank, width), f32),
            jax.ShapeDtypeStruct((1, rows, width), f32),
        ),
        in_specs=[local] * 4,
        out_specs=(anywhere,) * 2,
        scratch_shapes=[vmem((rank, width), f32), vmem((rows, width), f32), dma((5,))],
        compiler_params=pltpu.CompilerParams(vmem_limit_bytes=16 * 1024 * 1024),
    )(*(pltpu.with_memory_space_constraint(a, pltpu.VMEM) for a in passed))


def solution(mesh):
    nz = mesh.shape["dp"] // CORES
    nx = ny = {16: 4, 4: 2}[mesh.shape["tensor"]]
    placed = (P("dp", None), P("dp", "tensor"), P(None, "tensor"), P("dp", None, "tensor"))
    return jax.shard_map(
        functools.partial(on_device, nx, ny, nz),
        mesh=mesh,
        in_specs=placed,
        out_specs=(P(None, "tensor"), P("dp", None, "tensor")),
        check_vma=False,
    )
```

```python
import functools

import jax
import jax.numpy as jnp
from jax import lax
from jax.experimental import pallas as pl
from jax.experimental.pallas import tpu as pltpu
from jax.sharding import PartitionSpec as P

ridge_scale = 0.001
highest = lax.Precision.HIGHEST
f32 = jnp.float32
bf16 = jnp.bfloat16
MESH = pl.DeviceIdType.MESH
CORES = 2
FAR = {4: 5, 2: 1}


def dot(a, b, ca, cb, precision=None):
    return lax.dot_general(
        a, b, (((ca,), (cb,)), ((), ())), precision=precision, preferred_element_type=f32
    )


def split(value):
    high = value.astype(bf16)
    return high, (value - high.astype(f32)).astype(bf16)


def dot3(a, b, ca, cb):
    return dot(a[0], b[0], ca, cb) + (dot(a[0], b[1], ca, cb) + dot(a[1], b[0], ca, cb))


def await_bytes(ref, sem):
    pltpu.make_async_copy(ref, ref, sem).wait()


def ring_order(n):
    return sorted(range(1, n), key=lambda k: -min(k, n - k))


def kernel(
    nx, ny, nz,
    act_hbm, grad_hbm, q_hbm, err_hbm, merged, basis, n_all, inverse,
    act, grads, q_prev, err, part, from_core, half, xy_in, z_out, z_in, p_t,
    m_core, m_out, m_mate, m_pair, cross_out, cross_in, table,
    load_sem, core_send, core_recv, xy_send, xy_recv, z_send, z_recv, ag_send, ag_recv,
    fw_send, fw_recv, m_send, m_recv, mate_send, mate_recv, pair_send, pair_recv,
    cross_send, cross_recv, back_send, back_recv, known,
):
    rank, rows = p_t.shape
    width = merged.shape[1]
    nt = nx * ny
    half_rows = rows // CORES
    half_rank = rank // CORES
    block = rows // 4
    prank, pcols = half_rank // nx, rows // ny
    npair = nz // 2
    half_width = width // 2

    dp, t = lax.axis_index("dp"), lax.axis_index("tensor")
    z, c = lax.div(dp, CORES), lax.rem(dp, CORES)
    x, y = lax.div(t, ny), lax.rem(t, ny)
    odd = lax.rem(z, 2)
    mate = z + 1 - 2 * odd

    def device(z_at, c_at, x_at, y_at):
        return {"dp": z_at * CORES + c_at, "tensor": x_at * ny + y_at}

    def around(at, step, n):
        return lax.rem(at + step, n)

    def span(start, size):
        return pl.ds(pl.multiple_of(start, size), size)

    def send(src, dst, send_sem, recv_sem, to):
        pltpu.make_async_remote_copy(
            src_ref=src, dst_ref=dst, send_sem=send_sem, recv_sem=recv_sem,
            device_id=to, device_id_type=MESH,
        ).start()

    sibling = device(z, 1 - c, x, y)
    plane = sorted(
        ((dx, dy) for dx in range(nx) for dy in range(ny) if dx or dy),
        key=lambda d: -(min(d[0], nx - d[0]) + min(d[1], ny - d[1])),
    )
    far = [d for d in plane if min(d[0], nx - d[0]) + min(d[1], ny - d[1]) > nx // 2]
    near_plane = [d for d in plane if d not in far]
    ring = ring_order(nz)

    loads = [
        [pltpu.make_async_copy(grad_hbm, grads, load_sem.at[0]),
         pltpu.make_async_copy(q_hbm, q_prev, load_sem.at[1])]
    ]
    for k in range(4):
        at = pl.ds(k * block, block)
        loads.append([
            pltpu.make_async_copy(act_hbm.at[:, at], act.at[:, at], load_sem.at[2 + 2 * k]),
            pltpu.make_async_copy(err_hbm.at[0, at, :], err.at[at, :], load_sem.at[3 + 2 * k]),
        ])
    barrier = pltpu.get_barrier_semaphore()
    near = [dz for dz in ring if min(dz, nz - dz) <= nz // 4]
    greeted = [
        (min(dx, nx - dx) + min(dy, ny - dy), device(z, c, around(x, dx, nx), around(y, dy, ny)))
        for dx, dy in plane
    ]
    greeted += [(min(dz, nz - dz), device(around(z, dz, nz), c, x, y)) for dz in near]
    greeted += [
        (min(dx, nx - dx) + min(dy, ny - dy), device(z, 1 - c, around(x, dx, nx), around(y, dy, ny)))
        for dx, dy in far
    ]
    greeted += [(1, device(mate, 1 - c, x, y)), (0, sibling)]
    greeted.sort(key=lambda pair: -pair[0])

    def start(groups):
        for group in groups:
            for copy in group:
                copy.start()

    def greet(others):
        for other in others:
            pl.semaphore_signal(barrier, inc=1, device_id=other, device_id_type=MESH)

    start(loads[:2])
    greet([other for hops, other in greeted if hops > 2])
    start(loads[2:])
    greet([other for hops, other in greeted if hops <= 2])

    def gradient(k, carry):
        at = span(k * block, block)
        merged[at, :] = dot(act[:, at], grads[...], 0, 0) + err[at, :]
        return carry

    for copy in loads[0]:
        copy.wait()
    q_both = jnp.concatenate(split(q_prev[...]), axis=0)
    projected = dot(q_both, grads[...], 1, 1)
    projected = jnp.concatenate(split(projected[:rank] + projected[rank:]), axis=0)
    for k in range(4):
        at = pl.ds(k * block, block)
        for copy in loads[1 + k]:
            copy.wait()
        err_high, err_low = split(err[at, :])
        term = dot(projected, act[:, at], 1, 0) + dot(q_both, err_high, 1, 1)
        part[:, at] = (term[:rank] + term[rank:]) + dot(q_both[:rank], err_low, 1, 1)

    pl.semaphore_wait(barrier, len(greeted))

    own_ranks = span(c * half_rank, half_rank)
    send(part.at[span((1 - c) * half_rank, half_rank), :], from_core, core_send, core_recv, sibling)
    for k, (dx, dy) in enumerate(far):
        x_at, y_at = around(x, dx, nx), around(y, dy, ny)
        for c_at, slot in ((c, 0), (1 - c, 1)):
            rows_at = span(c_at * half_rank + x_at * prank, prank)
            send(part.at[rows_at, span(y_at * pcols, pcols)], xy_in.at[2 * k + slot],
                 xy_send, xy_recv, device(z, c_at, x_at, y_at))
    for dz in (nz // 4, nz - nz // 4):
        pl.semaphore_signal(
            known, inc=1, device_id=device(around(z, dz, nz), c, x, y), device_id_type=MESH
        )
    await_bytes(from_core, core_recv)
    half[...] = part[own_ranks, :] + from_core[...]

    def piece_of(ref, x_at, y_at):
        return ref.at[span(x_at * prank, prank), span(y_at * pcols, pcols)]

    for k, (dx, dy) in enumerate(near_plane):
        x_at, y_at = around(x, dx, nx), around(y, dy, ny)
        send(piece_of(half, x_at, y_at), xy_in.at[2 * len(far) + k],
             xy_send, xy_recv, device(z, c, x_at, y_at))
    arriving = nt - 1 + len(far)
    xy_in[arriving] = piece_of(half, x, y)[...]

    lax.fori_loop(0, 4, gradient, 0)
    own_rows = span(c * half_rows, half_rows)
    send(merged.at[span((1 - c) * half_rows, half_rows), :], m_core, m_send, m_recv, sibling)

    def to_mate():
        await_bytes(m_core, m_recv)
        there = span((1 - odd) * half_width, half_width)
        m_out[...] = merged[own_rows, there] + m_core[:, there]
        send(m_out, m_mate, mate_send, mate_recv, device(mate, c, x, y))
        here = span(odd * half_width, half_width)
        m_pair[own_rows, :] = merged[own_rows, here] + m_core[:, here]

    def to_sibling():
        await_bytes(m_mate, mate_recv)
        m_pair[own_rows, :] += m_mate[...]
        send(m_pair.at[own_rows, :], m_pair.at[own_rows, :], pair_send, pair_recv, sibling)

    await_bytes(xy_in.at[pl.ds(0, arriving)], xy_recv)
    piece = jnp.sum(xy_in[...], axis=0)
    z_out[...] = piece
    pl.semaphore_wait(known, 2)
    for dz in ring:
        send(z_out, z_in.at[z], z_send, z_recv, device(around(z, dz, nz), c, x, y))
    z_in[z] = piece

    to_mate()
    await_bytes(z_in.at[pl.ds(0, nz - 1)], z_recv)

    my_piece = p_t.at[span(c * half_rank + x * prank, prank), span(y * pcols, pcols)]
    my_piece[...] = jnp.sum(z_in[...], axis=0)

    for dx, dy in plane:
        send(my_piece, my_piece, ag_send, ag_recv.at[(ny - dy) % ny],
             device(z, c, around(x, dx, nx), around(y, dy, ny)))
    to_sibling()
    await_bytes(m_pair.at[pl.ds(0, half_rows), :], pair_recv)
    near_first = [0] + list(reversed(ring_order(ny)))
    terms = None
    for offset in near_first:
        count = (nx - 1 if offset == 0 else nx) * prank
        await_bytes(p_t.at[pl.ds(0, count), pl.ds(0, pcols)], ag_recv.at[offset])
        at = span(around(y, offset, ny) * pcols, pcols)
        ready = p_t.at[own_ranks, at]
        send(ready, ready, fw_send, fw_recv, sibling)
        term = dot3(split(ready[...]), split(m_pair[at, :]), 1, 0)
        terms = term if terms is None else terms + term
    cross_out[...] = terms

    pair_at = lax.div(z, 2)
    for dz in ring:
        if dz % 2 == 0:
            send(cross_out, cross_in.at[pair_at], cross_send, cross_recv,
                 device(around(z, dz, nz), c, x, y))
    cross_in[pair_at] = terms

    await_bytes(from_core, fw_recv)
    gram = dot(p_t[...], p_t[...], 1, 1, highest)
    row_at = lax.broadcasted_iota(jnp.int32, (rank, rank), 0)
    col_at = lax.broadcasted_iota(jnp.int32, (rank, rank), 1)
    eye = jnp.where(row_at == col_at, 1.0, 0.0).astype(f32)
    trace = jnp.sum(jnp.sum(gram * eye, axis=1, keepdims=True), axis=0, keepdims=True)
    shift = ridge_scale * rows * (trace / (rows * rank) + 1e-05)
    table[...] = jnp.concatenate([gram + shift * eye, eye], axis=1)
    rank_at = lax.broadcasted_iota(jnp.int32, (rank, 2 * rank), 0)

    def eliminate(k, held):
        for j in range(0, 8, 4):
            lines = [held[j + i : j + i + 1, :] for i in range(4)]
            square = [
                [jnp.broadcast_to(line[:, j + r : j + r + 1], line.shape) for r in range(4)]
                for line in lines
            ]
            scales = [jnp.broadcast_to(held[:, j + i : j + i + 1], held.shape) for i in range(4)]
            change = None
            for i in range(4):
                inv = 1.0 / square[i][i]
                below = (rank_at > j + i) & (rank_at < rank - 8 * k)
                scale = jnp.where(below, scales[i], 0.0)
                term = scale * (lines[i] * inv)
                change = term if change is None else change + term
                for l in range(i + 1, 4):
                    share = square[l][i] * inv
                    lines[l] = lines[l] - share * lines[i]
                    scales[l] = scales[l] - scale * (square[i][l] * inv)
                    for r in range(i + 1, 4):
                        square[l][r] = square[l][r] - share * square[i][r]
            held = held - change
        held = jnp.concatenate([held[8:], held[:8]], axis=0)
        return pltpu.roll(held, 2 * rank - 8, 1)

    table[...] = lax.fori_loop(0, rank // 8, eliminate, table[...])

    await_bytes(cross_in.at[pl.ds(0, npair - 1)], cross_recv)
    place = odd * CORES + c
    n_all[place] = jnp.sum(cross_in[...], axis=0)
    for z_at, c_at in ((mate, 1 - c), (mate, c), (z, 1 - c)):
        send(n_all.at[place], n_all.at[place], back_send, back_recv, device(z_at, c_at, x, y))

    pivots = jnp.sum(table[:, rank:] * eye, axis=1, keepdims=True)
    inverse[...] = table[:, :rank] * (1.0 / jnp.sqrt(pivots))

    def transposed(k, carry):
        at = span(k * block, block)
        high, low = split(p_t[:, at].T)
        basis[at, :] = jnp.concatenate([high, low, high, jnp.zeros_like(high)], axis=1)
        return carry

    lax.fori_loop(0, rows // block, transposed, 0)

    await_bytes(n_all.at[pl.ds(0, 3)], back_recv)
    await_bytes(from_core, core_send)
    await_bytes(xy_in.at[pl.ds(0, arriving)], xy_send)
    await_bytes(m_core, m_send)
    await_bytes(z_in.at[pl.ds(0, nz - 1)], z_send)
    await_bytes(m_mate, mate_send)
    await_bytes(m_pair.at[pl.ds(0, half_rows), :], pair_send)
    await_bytes(xy_in.at[pl.ds(0, nt - 1)], ag_send)
    await_bytes(from_core, fw_send)
    await_bytes(cross_in.at[pl.ds(0, npair - 1)], cross_send)
    await_bytes(n_all.at[pl.ds(0, 3)], back_send)


def finish(replicas, merged, basis, n_all, inverse, factor_hbm, res_hbm, factor, res, sems):
    rows = merged.shape[0]
    terms = jnp.concatenate([
        jnp.concatenate([n_all[k], n_all[CORES + k]], axis=1) for k in range(CORES)
    ], axis=0)
    factor[...] = dot(inverse[...], terms, 1, 0, highest) * (1.0 / replicas)
    out = pltpu.make_async_copy(factor, factor_hbm, sems.at[0])
    out.start()
    outs = [out]
    high, low = split(dot(inverse[...], factor[...], 0, 0, highest))
    back = jnp.concatenate([high, high, low, jnp.zeros_like(low)], axis=0)
    step = rows // 4
    for k in range(4):
        at = pl.ds(k * step, step)
        res[at, :] = merged[at, :] - dot(basis[at, :], back, 1, 0)
        outs.append(pltpu.make_async_copy(res.at[at, :], res_hbm.at[0, at, :], sems.at[1 + k]))
        outs[-1].start()
    for out in outs:
        out.wait()


def on_device(nx, ny, nz, activations, out_grads, q_previous, carried_error):
    tokens, rows = activations.shape
    width = out_grads.shape[1]
    rank = q_previous.shape[0]
    half_rows = rows // CORES
    half_rank, half_width = rank // CORES, width // 2
    piece = (half_rank // nx, rows // ny)
    columns = (half_rows, half_width)
    terms = (half_rank, half_width)
    vmem, dma = pltpu.VMEM, pltpu.SemaphoreType.DMA
    anywhere = pl.BlockSpec(memory_space=pl.ANY)
    local = pl.BlockSpec(memory_space=pltpu.VMEM)
    in_hbm = [
        pltpu.with_memory_space_constraint(a, pltpu.HBM)
        for a in (activations, out_grads, q_previous, carried_error)
    ]
    passed = pl.pallas_call(
        functools.partial(kernel, nx, ny, nz),
        name="powersgd",
        out_shape=(
            vmem((rows, width), f32),
            vmem((rows, 4 * rank), bf16),
            vmem((4, *terms), f32),
            vmem((rank, rank), f32),
        ),
        in_specs=[anywhere] * 4,
        out_specs=(local,) * 4,
        scratch_shapes=[
            vmem((tokens, rows), bf16),
            vmem((tokens, width), bf16),
            vmem((rank, width), f32),
            vmem((rows, width), f32),
            vmem((rank, rows), f32),
            vmem((half_rank, rows), f32),
            vmem((half_rank, rows), f32),
            vmem((nx * ny + FAR[nx], *piece), f32),
            vmem(piece, f32),
            vmem((nz, *piece), f32),
            vmem((rank, rows), f32),
            vmem((half_rows, width), f32),
            vmem(columns, f32),
            vmem(columns, f32),
            vmem((rows, half_width), f32),
            vmem(terms, f32),
            vmem((nz // 2, *terms), f32),
            vmem((rank, 2 * rank), f32),
            dma((10,)),
            dma, dma,
            dma, dma,
            dma, dma,
            dma, dma((ny,)),
            dma, dma,
            dma, dma,
            dma, dma,
            dma, dma,
            dma, dma,
            dma, dma,
            pltpu.SemaphoreType.REGULAR,
        ],
        compiler_params=pltpu.CompilerParams(
            collective_id=0, has_side_effects=True, vmem_limit_bytes=20 * 1024 * 1024
        ),
    )(*in_hbm)
    return pl.pallas_call(
        functools.partial(finish, nz * CORES),
        name="residual",
        out_shape=(
            jax.ShapeDtypeStruct((rank, width), f32),
            jax.ShapeDtypeStruct((1, rows, width), f32),
        ),
        in_specs=[local] * 4,
        out_specs=(anywhere,) * 2,
        scratch_shapes=[vmem((rank, width), f32), vmem((rows, width), f32), dma((5,))],
        compiler_params=pltpu.CompilerParams(vmem_limit_bytes=16 * 1024 * 1024),
    )(*(pltpu.with_memory_space_constraint(a, pltpu.VMEM) for a in passed))


def solution(mesh):
    nz = mesh.shape["dp"] // CORES
    nx = ny = {16: 4, 4: 2}[mesh.shape["tensor"]]
    placed = (P("dp", None), P("dp", "tensor"), P(None, "tensor"), P("dp", None, "tensor"))
    return jax.shard_map(
        functools.partial(on_device, nx, ny, nz),
        mesh=mesh,
        in_specs=placed,
        out_specs=(P(None, "tensor"), P("dp", None, "tensor")),
        check_vma=False,
    )
```

```python
import functools

import jax
import jax.numpy as jnp
from jax import lax
from jax.experimental import pallas as pl
from jax.experimental.pallas import tpu as pltpu
from jax.sharding import PartitionSpec as P

ridge_scale = 0.001
highest = lax.Precision.HIGHEST
f32 = jnp.float32
bf16 = jnp.bfloat16
MESH = pl.DeviceIdType.MESH
CORES = 2
FAR = {4: 5, 2: 1}


def dot(a, b, ca, cb, precision=None):
    return lax.dot_general(
        a, b, (((ca,), (cb,)), ((), ())), precision=precision, preferred_element_type=f32
    )


def split(value):
    high = value.astype(bf16)
    return high, (value - high.astype(f32)).astype(bf16)


def dot3(a, b, ca, cb):
    return dot(a[0], b[0], ca, cb) + (dot(a[0], b[1], ca, cb) + dot(a[1], b[0], ca, cb))


def await_bytes(ref, sem):
    pltpu.make_async_copy(ref, ref, sem).wait()


def ring_order(n):
    return sorted(range(1, n), key=lambda k: -min(k, n - k))


def kernel(
    nx, ny, nz,
    act_hbm, grad_hbm, q_hbm, err_hbm, merged, basis, n_all, inverse,
    act, grads, q_prev, err, part, from_core, half, xy_in, z_out, z_in, p_t,
    m_core, m_out, m_mate, m_pair, cross_out, cross_in, table,
    load_sem, core_send, core_recv, xy_send, xy_recv, z_send, z_recv, ag_send, ag_recv,
    fw_send, fw_recv, m_send, m_recv, mate_send, mate_recv, pair_send, pair_recv,
    cross_send, cross_recv, back_send, back_recv, known,
):
    rank, rows = p_t.shape
    width = merged.shape[1]
    nt = nx * ny
    half_rows = rows // CORES
    half_rank = rank // CORES
    block = rows // 4
    prank, pcols = half_rank // nx, rows // ny
    npair = nz // 2
    half_width = width // 2

    dp, t = lax.axis_index("dp"), lax.axis_index("tensor")
    z, c = lax.div(dp, CORES), lax.rem(dp, CORES)
    x, y = lax.div(t, ny), lax.rem(t, ny)
    odd = lax.rem(z, 2)
    mate = z + 1 - 2 * odd

    def device(z_at, c_at, x_at, y_at):
        return {"dp": z_at * CORES + c_at, "tensor": x_at * ny + y_at}

    def around(at, step, n):
        return lax.rem(at + step, n)

    def span(start, size):
        return pl.ds(pl.multiple_of(start, size), size)

    def send(src, dst, send_sem, recv_sem, to):
        pltpu.make_async_remote_copy(
            src_ref=src, dst_ref=dst, send_sem=send_sem, recv_sem=recv_sem,
            device_id=to, device_id_type=MESH,
        ).start()

    sibling = device(z, 1 - c, x, y)
    plane = sorted(
        ((dx, dy) for dx in range(nx) for dy in range(ny) if dx or dy),
        key=lambda d: -(min(d[0], nx - d[0]) + min(d[1], ny - d[1])),
    )
    far = [d for d in plane if min(d[0], nx - d[0]) + min(d[1], ny - d[1]) > nx // 2]
    near_plane = [d for d in plane if d not in far]
    ring = ring_order(nz)

    loads = [
        [pltpu.make_async_copy(grad_hbm, grads, load_sem.at[0]),
         pltpu.make_async_copy(q_hbm, q_prev, load_sem.at[1])]
    ]
    for k in range(4):
        at = pl.ds(k * block, block)
        loads.append([
            pltpu.make_async_copy(act_hbm.at[:, at], act.at[:, at], load_sem.at[2 + 2 * k]),
            pltpu.make_async_copy(err_hbm.at[0, at, :], err.at[at, :], load_sem.at[3 + 2 * k]),
        ])
    barrier = pltpu.get_barrier_semaphore()
    near = [dz for dz in ring if min(dz, nz - dz) <= nz // 4]
    greeted = [
        (min(dx, nx - dx) + min(dy, ny - dy), device(z, c, around(x, dx, nx), around(y, dy, ny)))
        for dx, dy in plane
    ]
    greeted += [(min(dz, nz - dz), device(around(z, dz, nz), c, x, y)) for dz in near]
    greeted += [
        (min(dx, nx - dx) + min(dy, ny - dy), device(z, 1 - c, around(x, dx, nx), around(y, dy, ny)))
        for dx, dy in far
    ]
    greeted += [(1, device(mate, 1 - c, x, y)), (0, sibling)]
    greeted.sort(key=lambda pair: -pair[0])

    for _, other in greeted:
        pl.semaphore_signal(barrier, inc=1, device_id=other, device_id_type=MESH)
    for group in loads:
        for copy in group:
            copy.start()

    def gradient(start):
        at = span(start, block)
        merged[at, :] = dot(act[:, at], grads[...], 0, 0) + err[at, :]

    for copy in loads[0]:
        copy.wait()
    q_both = jnp.concatenate(split(q_prev[...]), axis=0)
    projected = dot(q_both, grads[...], 1, 1)
    projected = jnp.concatenate(split(projected[:rank] + projected[rank:]), axis=0)
    for k in range(4):
        at = pl.ds(k * block, block)
        for copy in loads[1 + k]:
            copy.wait()
        err_high, err_low = split(err[at, :])
        term = dot(projected, act[:, at], 1, 0) + dot(q_both, err_high, 1, 1)
        part[:, at] = (term[:rank] + term[rank:]) + dot(q_both[:rank], err_low, 1, 1)

    pl.semaphore_wait(barrier, len(greeted))

    own_ranks = span(c * half_rank, half_rank)
    send(part.at[span((1 - c) * half_rank, half_rank), :], from_core, core_send, core_recv, sibling)
    for k, (dx, dy) in enumerate(far):
        x_at, y_at = around(x, dx, nx), around(y, dy, ny)
        for c_at, slot in ((c, 0), (1 - c, 1)):
            rows_at = span(c_at * half_rank + x_at * prank, prank)
            send(part.at[rows_at, span(y_at * pcols, pcols)], xy_in.at[2 * k + slot],
                 xy_send, xy_recv, device(z, c_at, x_at, y_at))
    for dz in (nz // 4, nz - nz // 4):
        pl.semaphore_signal(
            known, inc=1, device_id=device(around(z, dz, nz), c, x, y), device_id_type=MESH
        )
    gradient((1 - c) * half_rows)
    await_bytes(from_core, core_recv)
    half[...] = part[own_ranks, :] + from_core[...]

    def piece_of(ref, x_at, y_at):
        return ref.at[span(x_at * prank, prank), span(y_at * pcols, pcols)]

    for k, (dx, dy) in enumerate(near_plane):
        x_at, y_at = around(x, dx, nx), around(y, dy, ny)
        send(piece_of(half, x_at, y_at), xy_in.at[2 * len(far) + k],
             xy_send, xy_recv, device(z, c, x_at, y_at))
    arriving = nt - 1 + len(far)
    xy_in[arriving] = piece_of(half, x, y)[...]

    gradient((1 - c) * half_rows + block)
    own_rows = span(c * half_rows, half_rows)
    send(merged.at[span((1 - c) * half_rows, half_rows), :], m_core, m_send, m_recv, sibling)
    gradient(c * half_rows)
    gradient(c * half_rows + block)

    def to_mate():
        await_bytes(m_core, m_recv)
        there = span((1 - odd) * half_width, half_width)
        m_out[...] = merged[own_rows, there] + m_core[:, there]
        send(m_out, m_mate, mate_send, mate_recv, device(mate, c, x, y))
        here = span(odd * half_width, half_width)
        m_pair[own_rows, :] = merged[own_rows, here] + m_core[:, here]

    def to_sibling():
        await_bytes(m_mate, mate_recv)
        m_pair[own_rows, :] += m_mate[...]
        send(m_pair.at[own_rows, :], m_pair.at[own_rows, :], pair_send, pair_recv, sibling)

    await_bytes(xy_in.at[pl.ds(0, arriving)], xy_recv)
    piece = jnp.sum(xy_in[...], axis=0)
    z_out[...] = piece
    pl.semaphore_wait(known, 2)
    for dz in ring:
        send(z_out, z_in.at[z], z_send, z_recv, device(around(z, dz, nz), c, x, y))
    z_in[z] = piece

    to_mate()
    await_bytes(z_in.at[pl.ds(0, nz - 1)], z_recv)

    my_piece = p_t.at[span(c * half_rank + x * prank, prank), span(y * pcols, pcols)]
    my_piece[...] = jnp.sum(z_in[...], axis=0)

    for dx, dy in plane:
        send(my_piece, my_piece, ag_send, ag_recv.at[(ny - dy) % ny],
             device(z, c, around(x, dx, nx), around(y, dy, ny)))
    to_sibling()
    await_bytes(m_pair.at[pl.ds(0, half_rows), :], pair_recv)
    near_first = [0] + list(reversed(ring_order(ny)))
    terms = None
    for offset in near_first:
        count = (nx - 1 if offset == 0 else nx) * prank
        await_bytes(p_t.at[pl.ds(0, count), pl.ds(0, pcols)], ag_recv.at[offset])
        at = span(around(y, offset, ny) * pcols, pcols)
        ready = p_t.at[own_ranks, at]
        send(ready, ready, fw_send, fw_recv, sibling)
        term = dot3(split(ready[...]), split(m_pair[at, :]), 1, 0)
        terms = term if terms is None else terms + term
    cross_out[...] = terms

    pair_at = lax.div(z, 2)
    for dz in ring:
        if dz % 2 == 0:
            send(cross_out, cross_in.at[pair_at], cross_send, cross_recv,
                 device(around(z, dz, nz), c, x, y))
    cross_in[pair_at] = terms

    await_bytes(from_core, fw_recv)
    gram = dot(p_t[...], p_t[...], 1, 1, highest)
    row_at = lax.broadcasted_iota(jnp.int32, (rank, rank), 0)
    col_at = lax.broadcasted_iota(jnp.int32, (rank, rank), 1)
    eye = jnp.where(row_at == col_at, 1.0, 0.0).astype(f32)
    trace = jnp.sum(jnp.sum(gram * eye, axis=1, keepdims=True), axis=0, keepdims=True)
    shift = ridge_scale * rows * (trace / (rows * rank) + 1e-05)
    table[...] = jnp.concatenate([gram + shift * eye, eye], axis=1)
    rank_at = lax.broadcasted_iota(jnp.int32, (rank, 2 * rank), 0)

    def eliminate(k, held):
        for j in range(0, 8, 4):
            lines = [held[j + i : j + i + 1, :] for i in range(4)]
            square = [
                [jnp.broadcast_to(line[:, j + r : j + r + 1], line.shape) for r in range(4)]
                for line in lines
            ]
            scales = [jnp.broadcast_to(held[:, j + i : j + i + 1], held.shape) for i in range(4)]
            change = None
            for i in range(4):
                inv = 1.0 / square[i][i]
                below = (rank_at > j + i) & (rank_at < rank - 8 * k)
                scale = jnp.where(below, scales[i], 0.0)
                term = scale * (lines[i] * inv)
                change = term if change is None else change + term
                for l in range(i + 1, 4):
                    share = square[l][i] * inv
                    lines[l] = lines[l] - share * lines[i]
                    scales[l] = scales[l] - scale * (square[i][l] * inv)
                    for r in range(i + 1, 4):
                        square[l][r] = square[l][r] - share * square[i][r]
            held = held - change
        held = jnp.concatenate([held[8:], held[:8]], axis=0)
        return pltpu.roll(held, 2 * rank - 8, 1)

    table[...] = lax.fori_loop(0, rank // 8, eliminate, table[...])

    await_bytes(cross_in.at[pl.ds(0, npair - 1)], cross_recv)
    place = odd * CORES + c
    n_all[place] = jnp.sum(cross_in[...], axis=0)
    for z_at, c_at in ((mate, 1 - c), (mate, c), (z, 1 - c)):
        send(n_all.at[place], n_all.at[place], back_send, back_recv, device(z_at, c_at, x, y))

    pivots = jnp.sum(table[:, rank:] * eye, axis=1, keepdims=True)
    inverse[...] = table[:, :rank] * (1.0 / jnp.sqrt(pivots))

    def transposed(k, carry):
        at = span(k * block, block)
        high, low = split(p_t[:, at].T)
        basis[at, :] = jnp.concatenate([high, low, high, jnp.zeros_like(high)], axis=1)
        return carry

    lax.fori_loop(0, rows // block, transposed, 0)

    await_bytes(n_all.at[pl.ds(0, 3)], back_recv)
    await_bytes(from_core, core_send)
    await_bytes(xy_in.at[pl.ds(0, arriving)], xy_send)
    await_bytes(m_core, m_send)
    await_bytes(z_in.at[pl.ds(0, nz - 1)], z_send)
    await_bytes(m_mate, mate_send)
    await_bytes(m_pair.at[pl.ds(0, half_rows), :], pair_send)
    await_bytes(xy_in.at[pl.ds(0, nt - 1)], ag_send)
    await_bytes(from_core, fw_send)
    await_bytes(cross_in.at[pl.ds(0, npair - 1)], cross_send)
    await_bytes(n_all.at[pl.ds(0, 3)], back_send)


def finish(replicas, merged, basis, n_all, inverse, factor_hbm, res_hbm, factor, res, sems):
    terms = jnp.concatenate([
        jnp.concatenate([n_all[k], n_all[CORES + k]], axis=1) for k in range(CORES)
    ], axis=0)
    values = dot(inverse[...], terms, 1, 0, highest) * (1.0 / replicas)
    factor[...] = values
    high, low = split(dot(inverse[...], values, 0, 0, highest))
    back = jnp.concatenate([high, high, low, jnp.zeros_like(low)], axis=0)
    res[...] = merged[...] - dot(basis[...], back, 1, 0)
    outs = [
        pltpu.make_async_copy(res, res_hbm.at[0], sems.at[0]),
        pltpu.make_async_copy(factor, factor_hbm, sems.at[1]),
    ]
    for out in outs:
        out.start()
    for out in outs:
        out.wait()


def on_device(nx, ny, nz, activations, out_grads, q_previous, carried_error):
    tokens, rows = activations.shape
    width = out_grads.shape[1]
    rank = q_previous.shape[0]
    half_rows = rows // CORES
    half_rank, half_width = rank // CORES, width // 2
    piece = (half_rank // nx, rows // ny)
    columns = (half_rows, half_width)
    terms = (half_rank, half_width)
    vmem, dma = pltpu.VMEM, pltpu.SemaphoreType.DMA
    anywhere = pl.BlockSpec(memory_space=pl.ANY)
    local = pl.BlockSpec(memory_space=pltpu.VMEM)
    in_hbm = [
        pltpu.with_memory_space_constraint(a, pltpu.HBM)
        for a in (activations, out_grads, q_previous, carried_error)
    ]
    passed = pl.pallas_call(
        functools.partial(kernel, nx, ny, nz),
        name="powersgd",
        out_shape=(
            vmem((rows, width), f32),
            vmem((rows, 4 * rank), bf16),
            vmem((4, *terms), f32),
            vmem((rank, rank), f32),
        ),
        in_specs=[anywhere] * 4,
        out_specs=(local,) * 4,
        scratch_shapes=[
            vmem((tokens, rows), bf16),
            vmem((tokens, width), bf16),
            vmem((rank, width), f32),
            vmem((rows, width), f32),
            vmem((rank, rows), f32),
            vmem((half_rank, rows), f32),
            vmem((half_rank, rows), f32),
            vmem((nx * ny + FAR[nx], *piece), f32),
            vmem(piece, f32),
            vmem((nz, *piece), f32),
            vmem((rank, rows), f32),
            vmem((half_rows, width), f32),
            vmem(columns, f32),
            vmem(columns, f32),
            vmem((rows, half_width), f32),
            vmem(terms, f32),
            vmem((nz // 2, *terms), f32),
            vmem((rank, 2 * rank), f32),
            dma((10,)),
            dma, dma,
            dma, dma,
            dma, dma,
            dma, dma((ny,)),
            dma, dma,
            dma, dma,
            dma, dma,
            dma, dma,
            dma, dma,
            dma, dma,
            pltpu.SemaphoreType.REGULAR,
        ],
        compiler_params=pltpu.CompilerParams(
            collective_id=0, has_side_effects=True, vmem_limit_bytes=20 * 1024 * 1024
        ),
    )(*in_hbm)
    return pl.pallas_call(
        functools.partial(finish, nz * CORES),
        name="residual",
        out_shape=(
            jax.ShapeDtypeStruct((rank, width), f32),
            jax.ShapeDtypeStruct((1, rows, width), f32),
        ),
        in_specs=[local] * 4,
        out_specs=(anywhere,) * 2,
        scratch_shapes=[vmem((rank, width), f32), vmem((rows, width), f32), dma((2,))],
        compiler_params=pltpu.CompilerParams(vmem_limit_bytes=16 * 1024 * 1024),
    )(*(pltpu.with_memory_space_constraint(a, pltpu.VMEM) for a in passed))


def solution(mesh):
    nz = mesh.shape["dp"] // CORES
    nx = ny = {16: 4, 4: 2}[mesh.shape["tensor"]]
    placed = (P("dp", None), P("dp", "tensor"), P(None, "tensor"), P("dp", None, "tensor"))
    return jax.shard_map(
        functools.partial(on_device, nx, ny, nz),
        mesh=mesh,
        in_specs=placed,
        out_specs=(P(None, "tensor"), P("dp", None, "tensor")),
        check_vma=False,
    )
```

```python
import functools

import jax
import jax.numpy as jnp
from jax import lax
from jax.experimental import pallas as pl
from jax.experimental.pallas import tpu as pltpu
from jax.sharding import PartitionSpec as P

ridge_scale = 0.001
highest = lax.Precision.HIGHEST
f32 = jnp.float32
bf16 = jnp.bfloat16
MESH = pl.DeviceIdType.MESH
CORES = 2
FAR = {4: 5, 2: 1}


def dot(a, b, ca, cb, precision=None):
    return lax.dot_general(
        a, b, (((ca,), (cb,)), ((), ())), precision=precision, preferred_element_type=f32
    )


def split(value):
    high = value.astype(bf16)
    return high, (value - high.astype(f32)).astype(bf16)


def dot3(a, b, ca, cb):
    return dot(a[0], b[0], ca, cb) + (dot(a[0], b[1], ca, cb) + dot(a[1], b[0], ca, cb))


def await_bytes(ref, sem):
    pltpu.make_async_copy(ref, ref, sem).wait()


def ring_order(n):
    return sorted(range(1, n), key=lambda k: -min(k, n - k))


def kernel(
    nx, ny, nz,
    act_hbm, grad_hbm, q_hbm, err_hbm, merged, basis, n_all, inverse,
    act, grads, q_prev, err, part, from_core, half, xy_in, z_out, z_in, p_t,
    m_core, m_out, m_mate, m_pair, cross_out, cross_in, table,
    load_sem, core_send, core_recv, xy_send, xy_recv, z_send, z_recv, ag_send, ag_recv,
    fw_send, fw_recv, m_send, m_recv, mate_send, mate_recv, pair_send, pair_recv,
    cross_send, cross_recv, back_send, back_recv, known,
):
    rank, rows = p_t.shape
    width = merged.shape[1]
    nt = nx * ny
    half_rows = rows // CORES
    half_rank = rank // CORES
    block = rows // 4
    prank, pcols = half_rank // nx, rows // ny
    npair = nz // 2
    half_width = width // 2

    dp, t = lax.axis_index("dp"), lax.axis_index("tensor")
    z, c = lax.div(dp, CORES), lax.rem(dp, CORES)
    x, y = lax.div(t, ny), lax.rem(t, ny)
    odd = lax.rem(z, 2)
    mate = z + 1 - 2 * odd

    def device(z_at, c_at, x_at, y_at):
        return {"dp": z_at * CORES + c_at, "tensor": x_at * ny + y_at}

    def around(at, step, n):
        return lax.rem(at + step, n)

    def span(start, size):
        return pl.ds(pl.multiple_of(start, size), size)

    def send(src, dst, send_sem, recv_sem, to):
        pltpu.make_async_remote_copy(
            src_ref=src, dst_ref=dst, send_sem=send_sem, recv_sem=recv_sem,
            device_id=to, device_id_type=MESH,
        ).start()

    sibling = device(z, 1 - c, x, y)
    plane = sorted(
        ((dx, dy) for dx in range(nx) for dy in range(ny) if dx or dy),
        key=lambda d: -(min(d[0], nx - d[0]) + min(d[1], ny - d[1])),
    )
    far = [d for d in plane if min(d[0], nx - d[0]) + min(d[1], ny - d[1]) > nx // 2]
    near_plane = [d for d in plane if d not in far]
    ring = ring_order(nz)

    loads = [
        [pltpu.make_async_copy(grad_hbm, grads, load_sem.at[0]),
         pltpu.make_async_copy(q_hbm, q_prev, load_sem.at[1])]
    ]
    for k in range(4):
        at = pl.ds(k * block, block)
        loads.append([
            pltpu.make_async_copy(act_hbm.at[:, at], act.at[:, at], load_sem.at[2 + 2 * k]),
            pltpu.make_async_copy(err_hbm.at[0, at, :], err.at[at, :], load_sem.at[3 + 2 * k]),
        ])
    barrier = pltpu.get_barrier_semaphore()
    near = [dz for dz in ring if min(dz, nz - dz) <= nz // 4]
    greeted = [
        (min(dx, nx - dx) + min(dy, ny - dy), device(z, c, around(x, dx, nx), around(y, dy, ny)))
        for dx, dy in plane
    ]
    greeted += [(min(dz, nz - dz), device(around(z, dz, nz), c, x, y)) for dz in near]
    greeted += [
        (min(dx, nx - dx) + min(dy, ny - dy), device(z, 1 - c, around(x, dx, nx), around(y, dy, ny)))
        for dx, dy in far
    ]
    greeted += [(1, device(mate, 1 - c, x, y)), (0, sibling)]
    for _, other in sorted(greeted, key=lambda pair: -pair[0]):
        pl.semaphore_signal(barrier, inc=1, device_id=other, device_id_type=MESH)
    for group in loads:
        for copy in group:
            copy.start()

    def gradient(k, carry):
        at = span(k * block, block)
        merged[at, :] = dot(act[:, at], grads[...], 0, 0) + err[at, :]
        return carry

    for copy in loads[0]:
        copy.wait()
    q_both = jnp.concatenate(split(q_prev[...]), axis=0)
    projected = dot(q_both, grads[...], 1, 1)
    projected = jnp.concatenate(split(projected[:rank] + projected[rank:]), axis=0)
    for k in range(4):
        at = pl.ds(k * block, block)
        for copy in loads[1 + k]:
            copy.wait()
        err_high, err_low = split(err[at, :])
        term = dot(projected, act[:, at], 1, 0) + dot(q_both, err_high, 1, 1)
        part[:, at] = (term[:rank] + term[rank:]) + dot(q_both[:rank], err_low, 1, 1)

    pl.semaphore_wait(barrier, len(greeted))

    own_ranks = span(c * half_rank, half_rank)
    for k, (dx, dy) in enumerate(far):
        x_at, y_at = around(x, dx, nx), around(y, dy, ny)
        for c_at, slot in ((c, 0), (1 - c, 1)):
            rows_at = span(c_at * half_rank + x_at * prank, prank)
            send(part.at[rows_at, span(y_at * pcols, pcols)], xy_in.at[2 * k + slot],
                 xy_send, xy_recv, device(z, c_at, x_at, y_at))
    send(part.at[span((1 - c) * half_rank, half_rank), :], from_core, core_send, core_recv, sibling)
    for dz in (nz // 4, nz - nz // 4):
        pl.semaphore_signal(
            known, inc=1, device_id=device(around(z, dz, nz), c, x, y), device_id_type=MESH
        )
    await_bytes(from_core, core_recv)
    half[...] = part[own_ranks, :] + from_core[...]

    def piece_of(ref, x_at, y_at):
        return ref.at[span(x_at * prank, prank), span(y_at * pcols, pcols)]

    for k, (dx, dy) in enumerate(near_plane):
        x_at, y_at = around(x, dx, nx), around(y, dy, ny)
        send(piece_of(half, x_at, y_at), xy_in.at[2 * len(far) + k],
             xy_send, xy_recv, device(z, c, x_at, y_at))
    arriving = nt - 1 + len(far)
    xy_in[arriving] = piece_of(half, x, y)[...]

    lax.fori_loop(0, 4, gradient, 0)
    own_rows = span(c * half_rows, half_rows)
    send(merged.at[span((1 - c) * half_rows, half_rows), :], m_core, m_send, m_recv, sibling)

    def to_mate():
        await_bytes(m_core, m_recv)
        there = span((1 - odd) * half_width, half_width)
        m_out[...] = merged[own_rows, there] + m_core[:, there]
        send(m_out, m_mate, mate_send, mate_recv, device(mate, c, x, y))
        here = span(odd * half_width, half_width)
        m_pair[own_rows, :] = merged[own_rows, here] + m_core[:, here]

    def to_sibling():
        await_bytes(m_mate, mate_recv)
        m_pair[own_rows, :] += m_mate[...]
        send(m_pair.at[own_rows, :], m_pair.at[own_rows, :], pair_send, pair_recv, sibling)

    await_bytes(xy_in.at[pl.ds(0, arriving)], xy_recv)
    piece = jnp.sum(xy_in[...], axis=0)
    z_out[...] = piece
    pl.semaphore_wait(known, 2)
    for dz in ring:
        send(z_out, z_in.at[z], z_send, z_recv, device(around(z, dz, nz), c, x, y))
    z_in[z] = piece

    to_mate()
    await_bytes(z_in.at[pl.ds(0, nz - 1)], z_recv)

    my_piece = p_t.at[span(c * half_rank + x * prank, prank), span(y * pcols, pcols)]
    my_piece[...] = jnp.sum(z_in[...], axis=0)

    for dx, dy in plane:
        send(my_piece, my_piece, ag_send, ag_recv.at[(ny - dy) % ny],
             device(z, c, around(x, dx, nx), around(y, dy, ny)))
    to_sibling()
    await_bytes(m_pair.at[pl.ds(0, half_rows), :], pair_recv)
    near_first = [0] + list(reversed(ring_order(ny)))
    terms = None
    for offset in near_first:
        count = (nx - 1 if offset == 0 else nx) * prank
        await_bytes(p_t.at[pl.ds(0, count), pl.ds(0, pcols)], ag_recv.at[offset])
        at = span(around(y, offset, ny) * pcols, pcols)
        ready = p_t.at[own_ranks, at]
        send(ready, ready, fw_send, fw_recv, sibling)
        term = dot3(split(ready[...]), split(m_pair[at, :]), 1, 0)
        terms = term if terms is None else terms + term
    cross_out[...] = terms

    pair_at = lax.div(z, 2)
    for dz in ring:
        if dz % 2 == 0:
            send(cross_out, cross_in.at[pair_at], cross_send, cross_recv,
                 device(around(z, dz, nz), c, x, y))
    cross_in[pair_at] = terms

    await_bytes(from_core, fw_recv)
    gram = dot(p_t[...], p_t[...], 1, 1, highest)
    row_at = lax.broadcasted_iota(jnp.int32, (rank, rank), 0)
    col_at = lax.broadcasted_iota(jnp.int32, (rank, rank), 1)
    eye = jnp.where(row_at == col_at, 1.0, 0.0).astype(f32)
    trace = jnp.sum(jnp.sum(gram * eye, axis=1, keepdims=True), axis=0, keepdims=True)
    shift = ridge_scale * rows * (trace / (rows * rank) + 1e-05)
    table[...] = jnp.concatenate([gram + shift * eye, eye], axis=1)
    rank_at = lax.broadcasted_iota(jnp.int32, (rank, 2 * rank), 0)

    def eliminate(k, held):
        for j in range(0, 8, 4):
            lines = [held[j + i : j + i + 1, :] for i in range(4)]
            square = [
                [jnp.broadcast_to(line[:, j + r : j + r + 1], line.shape) for r in range(4)]
                for line in lines
            ]
            scales = [jnp.broadcast_to(held[:, j + i : j + i + 1], held.shape) for i in range(4)]
            change = None
            for i in range(4):
                inv = 1.0 / square[i][i]
                below = (rank_at > j + i) & (rank_at < rank - 8 * k)
                scale = jnp.where(below, scales[i], 0.0)
                term = scale * (lines[i] * inv)
                change = term if change is None else change + term
                for l in range(i + 1, 4):
                    share = square[l][i] * inv
                    lines[l] = lines[l] - share * lines[i]
                    scales[l] = scales[l] - scale * (square[i][l] * inv)
                    for r in range(i + 1, 4):
                        square[l][r] = square[l][r] - share * square[i][r]
            held = held - change
        held = jnp.concatenate([held[8:], held[:8]], axis=0)
        return pltpu.roll(held, 2 * rank - 8, 1)

    table[...] = lax.fori_loop(0, rank // 8, eliminate, table[...])

    await_bytes(cross_in.at[pl.ds(0, npair - 1)], cross_recv)
    place = odd * CORES + c
    n_all[place] = jnp.sum(cross_in[...], axis=0)
    for z_at, c_at in ((mate, 1 - c), (mate, c), (z, 1 - c)):
        send(n_all.at[place], n_all.at[place], back_send, back_recv, device(z_at, c_at, x, y))

    pivots = jnp.sum(table[:, rank:] * eye, axis=1, keepdims=True)
    inverse[...] = table[:, :rank] * (1.0 / jnp.sqrt(pivots))

    def transposed(k, carry):
        at = span(k * block, block)
        high, low = split(p_t[:, at].T)
        basis[at, :] = jnp.concatenate([high, low, high, jnp.zeros_like(high)], axis=1)
        return carry

    lax.fori_loop(0, rows // block, transposed, 0)

    await_bytes(n_all.at[pl.ds(0, 3)], back_recv)
    await_bytes(from_core, core_send)
    await_bytes(xy_in.at[pl.ds(0, arriving)], xy_send)
    await_bytes(m_core, m_send)
    await_bytes(z_in.at[pl.ds(0, nz - 1)], z_send)
    await_bytes(m_mate, mate_send)
    await_bytes(m_pair.at[pl.ds(0, half_rows), :], pair_send)
    await_bytes(xy_in.at[pl.ds(0, nt - 1)], ag_send)
    await_bytes(from_core, fw_send)
    await_bytes(cross_in.at[pl.ds(0, npair - 1)], cross_send)
    await_bytes(n_all.at[pl.ds(0, 3)], back_send)


def finish(replicas, merged, basis, n_all, inverse, factor_hbm, res_hbm, factor, res, sems):
    rows = merged.shape[0]
    terms = jnp.concatenate([
        jnp.concatenate([n_all[k], n_all[CORES + k]], axis=1) for k in range(CORES)
    ], axis=0)
    values = dot(inverse[...], terms, 1, 0, highest) * (1.0 / replicas)
    factor[...] = values
    high, low = split(dot(inverse[...], values, 0, 0, highest))
    back = jnp.concatenate([high, high, low, jnp.zeros_like(low)], axis=0)
    outs = []
    step = rows // 2
    for k in range(2):
        at = pl.ds(k * step, step)
        res[at, :] = merged[at, :] - dot(basis[at, :], back, 1, 0)
        outs.append(pltpu.make_async_copy(res.at[at, :], res_hbm.at[0, at, :], sems.at[k]))
        outs[-1].start()
    outs.append(pltpu.make_async_copy(factor, factor_hbm, sems.at[2]))
    outs[-1].start()
    for out in outs:
        out.wait()


def on_device(nx, ny, nz, activations, out_grads, q_previous, carried_error):
    tokens, rows = activations.shape
    width = out_grads.shape[1]
    rank = q_previous.shape[0]
    half_rows = rows // CORES
    half_rank, half_width = rank // CORES, width // 2
    piece = (half_rank // nx, rows // ny)
    columns = (half_rows, half_width)
    terms = (half_rank, half_width)
    vmem, dma = pltpu.VMEM, pltpu.SemaphoreType.DMA
    anywhere = pl.BlockSpec(memory_space=pl.ANY)
    local = pl.BlockSpec(memory_space=pltpu.VMEM)
    in_hbm = [
        pltpu.with_memory_space_constraint(a, pltpu.HBM)
        for a in (activations, out_grads, q_previous, carried_error)
    ]
    passed = pl.pallas_call(
        functools.partial(kernel, nx, ny, nz),
        name="powersgd",
        out_shape=(
            vmem((rows, width), f32),
            vmem((rows, 4 * rank), bf16),
            vmem((4, *terms), f32),
            vmem((rank, rank), f32),
        ),
        in_specs=[anywhere] * 4,
        out_specs=(local,) * 4,
        scratch_shapes=[
            vmem((tokens, rows), bf16),
            vmem((tokens, width), bf16),
            vmem((rank, width), f32),
            vmem((rows, width), f32),
            vmem((rank, rows), f32),
            vmem((half_rank, rows), f32),
            vmem((half_rank, rows), f32),
            vmem((nx * ny + FAR[nx], *piece), f32),
            vmem(piece, f32),
            vmem((nz, *piece), f32),
            vmem((rank, rows), f32),
            vmem((half_rows, width), f32),
            vmem(columns, f32),
            vmem(columns, f32),
            vmem((rows, half_width), f32),
            vmem(terms, f32),
            vmem((nz // 2, *terms), f32),
            vmem((rank, 2 * rank), f32),
            dma((10,)),
            dma, dma,
            dma, dma,
            dma, dma,
            dma, dma((ny,)),
            dma, dma,
            dma, dma,
            dma, dma,
            dma, dma,
            dma, dma,
            dma, dma,
            pltpu.SemaphoreType.REGULAR,
        ],
        compiler_params=pltpu.CompilerParams(
            collective_id=0, has_side_effects=True, vmem_limit_bytes=20 * 1024 * 1024
        ),
    )(*in_hbm)
    return pl.pallas_call(
        functools.partial(finish, nz * CORES),
        name="residual",
        out_shape=(
            jax.ShapeDtypeStruct((rank, width), f32),
            jax.ShapeDtypeStruct((1, rows, width), f32),
        ),
        in_specs=[local] * 4,
        out_specs=(anywhere,) * 2,
        scratch_shapes=[vmem((rank, width), f32), vmem((rows, width), f32), dma((3,))],
        compiler_params=pltpu.CompilerParams(vmem_limit_bytes=16 * 1024 * 1024),
    )(*(pltpu.with_memory_space_constraint(a, pltpu.VMEM) for a in passed))


def solution(mesh):
    nz = mesh.shape["dp"] // CORES
    nx = ny = {16: 4, 4: 2}[mesh.shape["tensor"]]
    placed = (P("dp", None), P("dp", "tensor"), P(None, "tensor"), P("dp", None, "tensor"))
    return jax.shard_map(
        functools.partial(on_device, nx, ny, nz),
        mesh=mesh,
        in_specs=placed,
        out_specs=(P(None, "tensor"), P("dp", None, "tensor")),
        check_vma=False,
    )
```

```python
import functools

import jax
import jax.numpy as jnp
from jax import lax
from jax.experimental import pallas as pl
from jax.experimental.pallas import tpu as pltpu
from jax.sharding import PartitionSpec as P

ridge_scale = 0.001
highest = lax.Precision.HIGHEST
f32 = jnp.float32
bf16 = jnp.bfloat16
MESH = pl.DeviceIdType.MESH
CORES = 2
FAR = {4: 5, 2: 1}


def dot(a, b, ca, cb, precision=None):
    return lax.dot_general(
        a, b, (((ca,), (cb,)), ((), ())), precision=precision, preferred_element_type=f32
    )


def split(value):
    high = value.astype(bf16)
    return high, (value - high.astype(f32)).astype(bf16)


def dot3(a, b, ca, cb):
    return dot(a[0], b[0], ca, cb) + (dot(a[0], b[1], ca, cb) + dot(a[1], b[0], ca, cb))


def await_bytes(ref, sem):
    pltpu.make_async_copy(ref, ref, sem).wait()


def ring_order(n):
    return sorted(range(1, n), key=lambda k: -min(k, n - k))


def kernel(
    nx, ny, nz,
    act_hbm, grad_hbm, q_hbm, err_hbm, merged, basis, n_all, inverse,
    act, grads, q_prev, err, part, from_core, half, xy_in, z_out, z_in, p_t,
    m_core, m_out, m_mate, m_pair, cross_out, cross_in, table,
    load_sem, core_send, core_recv, xy_send, xy_recv, z_send, z_recv, ag_send, ag_recv,
    fw_send, fw_recv, m_send, m_recv, mate_send, mate_recv, pair_send, pair_recv,
    cross_send, cross_recv, back_send, back_recv, known,
):
    rank, rows = p_t.shape
    width = merged.shape[1]
    nt = nx * ny
    half_rows = rows // CORES
    half_rank = rank // CORES
    block = rows // 4
    prank, pcols = half_rank // nx, rows // ny
    npair = nz // 2
    half_width = width // 2

    dp, t = lax.axis_index("dp"), lax.axis_index("tensor")
    z, c = lax.div(dp, CORES), lax.rem(dp, CORES)
    x, y = lax.div(t, ny), lax.rem(t, ny)
    odd = lax.rem(z, 2)
    mate = z + 1 - 2 * odd

    def device(z_at, c_at, x_at, y_at):
        return {"dp": z_at * CORES + c_at, "tensor": x_at * ny + y_at}

    def around(at, step, n):
        return lax.rem(at + step, n)

    def span(start, size):
        return pl.ds(pl.multiple_of(start, size), size)

    def send(src, dst, send_sem, recv_sem, to):
        pltpu.make_async_remote_copy(
            src_ref=src, dst_ref=dst, send_sem=send_sem, recv_sem=recv_sem,
            device_id=to, device_id_type=MESH,
        ).start()

    sibling = device(z, 1 - c, x, y)
    plane = sorted(
        ((dx, dy) for dx in range(nx) for dy in range(ny) if dx or dy),
        key=lambda d: -(min(d[0], nx - d[0]) + min(d[1], ny - d[1])),
    )
    far = [d for d in plane if min(d[0], nx - d[0]) + min(d[1], ny - d[1]) > nx // 2]
    near_plane = [d for d in plane if d not in far]
    ring = ring_order(nz)

    loads = [
        [pltpu.make_async_copy(grad_hbm, grads, load_sem.at[0]),
         pltpu.make_async_copy(q_hbm, q_prev, load_sem.at[1])]
    ]
    for k in range(4):
        at = pl.ds(k * block, block)
        loads.append([
            pltpu.make_async_copy(act_hbm.at[:, at], act.at[:, at], load_sem.at[2 + 2 * k]),
            pltpu.make_async_copy(err_hbm.at[0, at, :], err.at[at, :], load_sem.at[3 + 2 * k]),
        ])
    barrier = pltpu.get_barrier_semaphore()
    near = [dz for dz in ring if min(dz, nz - dz) <= 2]
    greeted = [
        (min(dx, nx - dx) + min(dy, ny - dy), device(z, c, around(x, dx, nx), around(y, dy, ny)))
        for dx, dy in plane
    ]
    greeted += [(min(dz, nz - dz), device(around(z, dz, nz), c, x, y)) for dz in near]
    greeted += [
        (min(dx, nx - dx) + min(dy, ny - dy), device(z, 1 - c, around(x, dx, nx), around(y, dy, ny)))
        for dx, dy in far
    ]
    greeted += [(1, device(mate, 1 - c, x, y)), (0, sibling)]
    for _, other in sorted(greeted, key=lambda pair: -pair[0]):
        pl.semaphore_signal(barrier, inc=1, device_id=other, device_id_type=MESH)
    for group in loads:
        for copy in group:
            copy.start()

    def gradient(k, carry):
        at = span(k * block, block)
        merged[at, :] = dot(act[:, at], grads[...], 0, 0) + err[at, :]
        return carry

    for copy in loads[0]:
        copy.wait()
    q_both = jnp.concatenate(split(q_prev[...]), axis=0)
    projected = dot(q_both, grads[...], 1, 1)
    projected = jnp.concatenate(split(projected[:rank] + projected[rank:]), axis=0)
    for k in range(4):
        at = pl.ds(k * block, block)
        for copy in loads[1 + k]:
            copy.wait()
        err_high, err_low = split(err[at, :])
        term = dot(projected, act[:, at], 1, 0) + dot(q_both, err_high, 1, 1)
        part[:, at] = (term[:rank] + term[rank:]) + dot(q_both[:rank], err_low, 1, 1)

    pl.semaphore_wait(barrier, len(greeted))

    own_ranks = span(c * half_rank, half_rank)
    for k, (dx, dy) in enumerate(far):
        x_at, y_at = around(x, dx, nx), around(y, dy, ny)
        for c_at, slot in ((c, 0), (1 - c, 1)):
            rows_at = span(c_at * half_rank + x_at * prank, prank)
            send(part.at[rows_at, span(y_at * pcols, pcols)], xy_in.at[2 * k + slot],
                 xy_send, xy_recv, device(z, c_at, x_at, y_at))
    send(part.at[span((1 - c) * half_rank, half_rank), :], from_core, core_send, core_recv, sibling)
    reach = 2

    def pass_on(stage):
        if stage > 0:
            pl.semaphore_wait(known.at[stage - 1], 2)
        for dz in (reach, nz - reach):
            pl.semaphore_signal(
                known.at[stage], inc=1, device_id=device(around(z, dz, nz), c, x, y),
                device_id_type=MESH,
            )

    pass_on(0)
    await_bytes(from_core, core_recv)
    half[...] = part[own_ranks, :] + from_core[...]

    def piece_of(ref, x_at, y_at):
        return ref.at[span(x_at * prank, prank), span(y_at * pcols, pcols)]

    for k, (dx, dy) in enumerate(near_plane):
        x_at, y_at = around(x, dx, nx), around(y, dy, ny)
        send(piece_of(half, x_at, y_at), xy_in.at[2 * len(far) + k],
             xy_send, xy_recv, device(z, c, x_at, y_at))
    pass_on(1)
    arriving = nt - 1 + len(far)
    xy_in[arriving] = piece_of(half, x, y)[...]

    lax.fori_loop(0, 2, gradient, 0)
    pass_on(2)
    lax.fori_loop(2, 4, gradient, 0)
    own_rows = span(c * half_rows, half_rows)
    send(merged.at[span((1 - c) * half_rows, half_rows), :], m_core, m_send, m_recv, sibling)

    def to_mate():
        await_bytes(m_core, m_recv)
        there = span((1 - odd) * half_width, half_width)
        m_out[...] = merged[own_rows, there] + m_core[:, there]
        send(m_out, m_mate, mate_send, mate_recv, device(mate, c, x, y))
        here = span(odd * half_width, half_width)
        m_pair[own_rows, :] = merged[own_rows, here] + m_core[:, here]

    def to_sibling():
        await_bytes(m_mate, mate_recv)
        m_pair[own_rows, :] += m_mate[...]
        send(m_pair.at[own_rows, :], m_pair.at[own_rows, :], pair_send, pair_recv, sibling)

    await_bytes(xy_in.at[pl.ds(0, arriving)], xy_recv)
    piece = jnp.sum(xy_in[...], axis=0)
    z_out[...] = piece
    pl.semaphore_wait(known.at[2], 2)
    for dz in ring:
        send(z_out, z_in.at[z], z_send, z_recv, device(around(z, dz, nz), c, x, y))
    z_in[z] = piece

    to_mate()
    await_bytes(z_in.at[pl.ds(0, nz - 1)], z_recv)

    my_piece = p_t.at[span(c * half_rank + x * prank, prank), span(y * pcols, pcols)]
    my_piece[...] = jnp.sum(z_in[...], axis=0)

    for dx, dy in plane:
        send(my_piece, my_piece, ag_send, ag_recv.at[(ny - dy) % ny],
             device(z, c, around(x, dx, nx), around(y, dy, ny)))
    to_sibling()
    await_bytes(m_pair.at[pl.ds(0, half_rows), :], pair_recv)
    near_first = [0] + list(reversed(ring_order(ny)))
    terms = None
    for offset in near_first:
        count = (nx - 1 if offset == 0 else nx) * prank
        await_bytes(p_t.at[pl.ds(0, count), pl.ds(0, pcols)], ag_recv.at[offset])
        at = span(around(y, offset, ny) * pcols, pcols)
        ready = p_t.at[own_ranks, at]
        send(ready, ready, fw_send, fw_recv, sibling)
        term = dot3(split(ready[...]), split(m_pair[at, :]), 1, 0)
        terms = term if terms is None else terms + term
    cross_out[...] = terms

    pair_at = lax.div(z, 2)
    for dz in ring:
        if dz % 2 == 0:
            send(cross_out, cross_in.at[pair_at], cross_send, cross_recv,
                 device(around(z, dz, nz), c, x, y))
    cross_in[pair_at] = terms

    await_bytes(from_core, fw_recv)
    gram = dot(p_t[...], p_t[...], 1, 1, highest)
    row_at = lax.broadcasted_iota(jnp.int32, (rank, rank), 0)
    col_at = lax.broadcasted_iota(jnp.int32, (rank, rank), 1)
    eye = jnp.where(row_at == col_at, 1.0, 0.0).astype(f32)
    trace = jnp.sum(jnp.sum(gram * eye, axis=1, keepdims=True), axis=0, keepdims=True)
    shift = ridge_scale * rows * (trace / (rows * rank) + 1e-05)
    table[...] = jnp.concatenate([gram + shift * eye, eye], axis=1)
    rank_at = lax.broadcasted_iota(jnp.int32, (rank, 2 * rank), 0)

    def eliminate(k, held):
        for j in range(0, 8, 4):
            lines = [held[j + i : j + i + 1, :] for i in range(4)]
            square = [
                [jnp.broadcast_to(line[:, j + r : j + r + 1], line.shape) for r in range(4)]
                for line in lines
            ]
            scales = [jnp.broadcast_to(held[:, j + i : j + i + 1], held.shape) for i in range(4)]
            change = None
            for i in range(4):
                inv = 1.0 / square[i][i]
                below = (rank_at > j + i) & (rank_at < rank - 8 * k)
                scale = jnp.where(below, scales[i], 0.0)
                term = scale * (lines[i] * inv)
                change = term if change is None else change + term
                for l in range(i + 1, 4):
                    share = square[l][i] * inv
                    lines[l] = lines[l] - share * lines[i]
                    scales[l] = scales[l] - scale * (square[i][l] * inv)
                    for r in range(i + 1, 4):
                        square[l][r] = square[l][r] - share * square[i][r]
            held = held - change
        held = jnp.concatenate([held[8:], held[:8]], axis=0)
        return pltpu.roll(held, 2 * rank - 8, 1)

    table[...] = lax.fori_loop(0, rank // 8, eliminate, table[...])

    await_bytes(cross_in.at[pl.ds(0, npair - 1)], cross_recv)
    place = odd * CORES + c
    n_all[place] = jnp.sum(cross_in[...], axis=0)
    for z_at, c_at in ((mate, 1 - c), (mate, c), (z, 1 - c)):
        send(n_all.at[place], n_all.at[place], back_send, back_recv, device(z_at, c_at, x, y))

    pivots = jnp.sum(table[:, rank:] * eye, axis=1, keepdims=True)
    inverse[...] = table[:, :rank] * (1.0 / jnp.sqrt(pivots))

    def transposed(k, carry):
        at = span(k * block, block)
        high, low = split(p_t[:, at].T)
        basis[at, :] = jnp.concatenate([high, low, high, jnp.zeros_like(high)], axis=1)
        return carry

    lax.fori_loop(0, rows // block, transposed, 0)

    await_bytes(n_all.at[pl.ds(0, 3)], back_recv)
    await_bytes(from_core, core_send)
    await_bytes(xy_in.at[pl.ds(0, arriving)], xy_send)
    await_bytes(m_core, m_send)
    await_bytes(z_in.at[pl.ds(0, nz - 1)], z_send)
    await_bytes(m_mate, mate_send)
    await_bytes(m_pair.at[pl.ds(0, half_rows), :], pair_send)
    await_bytes(xy_in.at[pl.ds(0, nt - 1)], ag_send)
    await_bytes(from_core, fw_send)
    await_bytes(cross_in.at[pl.ds(0, npair - 1)], cross_send)
    await_bytes(n_all.at[pl.ds(0, 3)], back_send)


def finish(replicas, merged, basis, n_all, inverse, factor_hbm, res_hbm, factor, res, sems):
    rows = merged.shape[0]
    terms = jnp.concatenate([
        jnp.concatenate([n_all[k], n_all[CORES + k]], axis=1) for k in range(CORES)
    ], axis=0)
    values = dot(inverse[...], terms, 1, 0, highest) * (1.0 / replicas)
    factor[...] = values
    high, low = split(dot(inverse[...], values, 0, 0, highest))
    back = jnp.concatenate([high, high, low, jnp.zeros_like(low)], axis=0)
    outs = []
    step = rows // 2
    for k in range(2):
        at = pl.ds(k * step, step)
        res[at, :] = merged[at, :] - dot(basis[at, :], back, 1, 0)
        outs.append(pltpu.make_async_copy(res.at[at, :], res_hbm.at[0, at, :], sems.at[k]))
        outs[-1].start()
    outs.append(pltpu.make_async_copy(factor, factor_hbm, sems.at[2]))
    outs[-1].start()
    for out in outs:
        out.wait()


def on_device(nx, ny, nz, activations, out_grads, q_previous, carried_error):
    tokens, rows = activations.shape
    width = out_grads.shape[1]
    rank = q_previous.shape[0]
    half_rows = rows // CORES
    half_rank, half_width = rank // CORES, width // 2
    piece = (half_rank // nx, rows // ny)
    columns = (half_rows, half_width)
    terms = (half_rank, half_width)
    vmem, dma = pltpu.VMEM, pltpu.SemaphoreType.DMA
    anywhere = pl.BlockSpec(memory_space=pl.ANY)
    local = pl.BlockSpec(memory_space=pltpu.VMEM)
    in_hbm = [
        pltpu.with_memory_space_constraint(a, pltpu.HBM)
        for a in (activations, out_grads, q_previous, carried_error)
    ]
    passed = pl.pallas_call(
        functools.partial(kernel, nx, ny, nz),
        name="powersgd",
        out_shape=(
            vmem((rows, width), f32),
            vmem((rows, 4 * rank), bf16),
            vmem((4, *terms), f32),
            vmem((rank, rank), f32),
        ),
        in_specs=[anywhere] * 4,
        out_specs=(local,) * 4,
        scratch_shapes=[
            vmem((tokens, rows), bf16),
            vmem((tokens, width), bf16),
            vmem((rank, width), f32),
            vmem((rows, width), f32),
            vmem((rank, rows), f32),
            vmem((half_rank, rows), f32),
            vmem((half_rank, rows), f32),
            vmem((nx * ny + FAR[nx], *piece), f32),
            vmem(piece, f32),
            vmem((nz, *piece), f32),
            vmem((rank, rows), f32),
            vmem((half_rows, width), f32),
            vmem(columns, f32),
            vmem(columns, f32),
            vmem((rows, half_width), f32),
            vmem(terms, f32),
            vmem((nz // 2, *terms), f32),
            vmem((rank, 2 * rank), f32),
            dma((10,)),
            dma, dma,
            dma, dma,
            dma, dma,
            dma, dma((ny,)),
            dma, dma,
            dma, dma,
            dma, dma,
            dma, dma,
            dma, dma,
            dma, dma,
            pltpu.SemaphoreType.REGULAR((3,)),
        ],
        compiler_params=pltpu.CompilerParams(
            collective_id=0, has_side_effects=True, vmem_limit_bytes=20 * 1024 * 1024
        ),
    )(*in_hbm)
    return pl.pallas_call(
        functools.partial(finish, nz * CORES),
        name="residual",
        out_shape=(
            jax.ShapeDtypeStruct((rank, width), f32),
            jax.ShapeDtypeStruct((1, rows, width), f32),
        ),
        in_specs=[local] * 4,
        out_specs=(anywhere,) * 2,
        scratch_shapes=[vmem((rank, width), f32), vmem((rows, width), f32), dma((3,))],
        compiler_params=pltpu.CompilerParams(vmem_limit_bytes=16 * 1024 * 1024),
    )(*(pltpu.with_memory_space_constraint(a, pltpu.VMEM) for a in passed))


def solution(mesh):
    nz = mesh.shape["dp"] // CORES
    nx = ny = {16: 4, 4: 2}[mesh.shape["tensor"]]
    placed = (P("dp", None), P("dp", "tensor"), P(None, "tensor"), P("dp", None, "tensor"))
    return jax.shard_map(
        functools.partial(on_device, nx, ny, nz),
        mesh=mesh,
        in_specs=placed,
        out_specs=(P(None, "tensor"), P("dp", None, "tensor")),
        check_vma=False,
    )
```

```python
import functools

import jax
import jax.numpy as jnp
from jax import lax
from jax.experimental import pallas as pl
from jax.experimental.pallas import tpu as pltpu
from jax.sharding import PartitionSpec as P

ridge_scale = 0.001
highest = lax.Precision.HIGHEST
f32 = jnp.float32
bf16 = jnp.bfloat16
MESH = pl.DeviceIdType.MESH
CORES = 2
FAR = {4: 5, 2: 1}


def dot(a, b, ca, cb, precision=None):
    return lax.dot_general(
        a, b, (((ca,), (cb,)), ((), ())), precision=precision, preferred_element_type=f32
    )


def split(value):
    high = value.astype(bf16)
    return high, (value - high.astype(f32)).astype(bf16)


def dot3(a, b, ca, cb):
    return dot(a[0], b[0], ca, cb) + (dot(a[0], b[1], ca, cb) + dot(a[1], b[0], ca, cb))


def await_bytes(ref, sem):
    pltpu.make_async_copy(ref, ref, sem).wait()


def ring_order(n):
    return sorted(range(1, n), key=lambda k: -min(k, n - k))


def kernel(
    nx, ny, nz,
    act_hbm, grad_hbm, q_hbm, err_hbm, merged, basis, n_all, inverse,
    act, grads, q_prev, err, part, from_core, half, xy_in, z_out, z_in, p_t,
    m_core, m_out, m_mate, m_pair, cross_out, cross_in, table,
    load_sem, core_send, core_recv, xy_send, xy_recv, z_send, z_recv, ag_send, ag_recv,
    fw_send, fw_recv, m_send, m_recv, mate_send, mate_recv, pair_send, pair_recv,
    cross_send, cross_recv, back_send, back_recv, known,
):
    rank, rows = p_t.shape
    width = merged.shape[1]
    nt = nx * ny
    half_rows = rows // CORES
    half_rank = rank // CORES
    block = rows // 4
    prank, pcols = half_rank // nx, rows // ny
    npair = nz // 2
    half_width = width // 2

    dp, t = lax.axis_index("dp"), lax.axis_index("tensor")
    z, c = lax.div(dp, CORES), lax.rem(dp, CORES)
    x, y = lax.div(t, ny), lax.rem(t, ny)
    odd = lax.rem(z, 2)
    mate = z + 1 - 2 * odd

    def device(z_at, c_at, x_at, y_at):
        return {"dp": z_at * CORES + c_at, "tensor": x_at * ny + y_at}

    def around(at, step, n):
        return lax.rem(at + step, n)

    def span(start, size):
        return pl.ds(pl.multiple_of(start, size), size)

    def send(src, dst, send_sem, recv_sem, to):
        pltpu.make_async_remote_copy(
            src_ref=src, dst_ref=dst, send_sem=send_sem, recv_sem=recv_sem,
            device_id=to, device_id_type=MESH,
        ).start()

    sibling = device(z, 1 - c, x, y)
    plane = sorted(
        ((dx, dy) for dx in range(nx) for dy in range(ny) if dx or dy),
        key=lambda d: -(min(d[0], nx - d[0]) + min(d[1], ny - d[1])),
    )
    far = [d for d in plane if min(d[0], nx - d[0]) + min(d[1], ny - d[1]) > nx // 2]
    near_plane = [d for d in plane if d not in far]
    ring = ring_order(nz)

    loads = [
        [pltpu.make_async_copy(grad_hbm, grads, load_sem.at[0]),
         pltpu.make_async_copy(q_hbm, q_prev, load_sem.at[1])]
    ]
    for k in range(4):
        at = pl.ds(k * block, block)
        loads.append([
            pltpu.make_async_copy(act_hbm.at[:, at], act.at[:, at], load_sem.at[2 + 2 * k]),
            pltpu.make_async_copy(err_hbm.at[0, at, :], err.at[at, :], load_sem.at[3 + 2 * k]),
        ])
    barrier = pltpu.get_barrier_semaphore()
    near = [dz for dz in ring if min(dz, nz - dz) <= 2]
    greeted = [
        (min(dx, nx - dx) + min(dy, ny - dy), device(z, c, around(x, dx, nx), around(y, dy, ny)))
        for dx, dy in plane
    ]
    greeted += [(min(dz, nz - dz), device(around(z, dz, nz), c, x, y)) for dz in near]
    greeted += [
        (min(dx, nx - dx) + min(dy, ny - dy), device(z, 1 - c, around(x, dx, nx), around(y, dy, ny)))
        for dx, dy in far
    ]
    greeted += [(1, device(mate, 1 - c, x, y)), (0, sibling)]
    for _, other in sorted(greeted, key=lambda pair: -pair[0]):
        pl.semaphore_signal(barrier, inc=1, device_id=other, device_id_type=MESH)
    for group in loads:
        for copy in group:
            copy.start()

    def gradient(k, carry):
        at = span(k * block, block)
        merged[at, :] = dot(act[:, at], grads[...], 0, 0) + err[at, :]
        return carry

    for copy in loads[0]:
        copy.wait()
    q_both = jnp.concatenate(split(q_prev[...]), axis=0)
    projected = dot(q_both, grads[...], 1, 1)
    projected = jnp.concatenate(split(projected[:rank] + projected[rank:]), axis=0)
    for k in range(4):
        at = pl.ds(k * block, block)
        for copy in loads[1 + k]:
            copy.wait()
        err_high, err_low = split(err[at, :])
        term = dot(projected, act[:, at], 1, 0) + dot(q_both, err_high, 1, 1)
        part[:, at] = (term[:rank] + term[rank:]) + dot(q_both[:rank], err_low, 1, 1)

    pl.semaphore_wait(barrier, len(greeted))

    own_ranks = span(c * half_rank, half_rank)
    for k, (dx, dy) in enumerate(far):
        x_at, y_at = around(x, dx, nx), around(y, dy, ny)
        for c_at, slot in ((c, 0), (1 - c, 1)):
            rows_at = span(c_at * half_rank + x_at * prank, prank)
            send(part.at[rows_at, span(y_at * pcols, pcols)], xy_in.at[2 * k + slot],
                 xy_send, xy_recv, device(z, c_at, x_at, y_at))
    send(part.at[span((1 - c) * half_rank, half_rank), :], from_core, core_send, core_recv, sibling)
    reach = 2

    def pass_on(stage):
        if stage > 0:
            pl.semaphore_wait(known.at[stage - 1], 2)
        for dz in (reach, nz - reach):
            pl.semaphore_signal(
                known.at[stage], inc=1, device_id=device(around(z, dz, nz), c, x, y),
                device_id_type=MESH,
            )

    pass_on(0)
    await_bytes(from_core, core_recv)
    half[...] = part[own_ranks, :] + from_core[...]

    def piece_of(ref, x_at, y_at):
        return ref.at[span(x_at * prank, prank), span(y_at * pcols, pcols)]

    for k, (dx, dy) in enumerate(near_plane):
        x_at, y_at = around(x, dx, nx), around(y, dy, ny)
        send(piece_of(half, x_at, y_at), xy_in.at[2 * len(far) + k],
             xy_send, xy_recv, device(z, c, x_at, y_at))
    pass_on(1)
    arriving = nt - 1 + len(far)
    xy_in[arriving] = piece_of(half, x, y)[...]

    lax.fori_loop(0, 2, gradient, 0)
    pass_on(2)
    lax.fori_loop(2, 4, gradient, 0)
    own_rows = span(c * half_rows, half_rows)
    send(merged.at[span((1 - c) * half_rows, half_rows), :], m_core, m_send, m_recv, sibling)

    def to_mate():
        await_bytes(m_core, m_recv)
        there = span((1 - odd) * half_width, half_width)
        m_out[...] = merged[own_rows, there] + m_core[:, there]
        send(m_out, m_mate, mate_send, mate_recv, device(mate, c, x, y))
        here = span(odd * half_width, half_width)
        m_pair[own_rows, :] = merged[own_rows, here] + m_core[:, here]

    def to_sibling():
        await_bytes(m_mate, mate_recv)
        m_pair[own_rows, :] += m_mate[...]
        send(m_pair.at[own_rows, :], m_pair.at[own_rows, :], pair_send, pair_recv, sibling)

    await_bytes(xy_in.at[pl.ds(0, arriving)], xy_recv)
    piece = jnp.sum(xy_in[...], axis=0)
    z_out[...] = piece
    pl.semaphore_wait(known.at[2], 2)
    for dz in ring:
        send(z_out, z_in.at[z], z_send, z_recv, device(around(z, dz, nz), c, x, y))
    z_in[z] = piece

    to_mate()
    await_bytes(z_in.at[pl.ds(0, nz - 1)], z_recv)

    my_piece = p_t.at[span(c * half_rank + x * prank, prank), span(y * pcols, pcols)]
    my_piece[...] = jnp.sum(z_in[...], axis=0)

    for dx, dy in plane:
        send(my_piece, my_piece, ag_send, ag_recv.at[(ny - dy) % ny],
             device(z, c, around(x, dx, nx), around(y, dy, ny)))
    to_sibling()
    await_bytes(m_pair.at[pl.ds(0, half_rows), :], pair_recv)
    near_first = [0] + list(reversed(ring_order(ny)))
    terms = None
    for offset in near_first:
        count = (nx - 1 if offset == 0 else nx) * prank
        await_bytes(p_t.at[pl.ds(0, count), pl.ds(0, pcols)], ag_recv.at[offset])
        at = span(around(y, offset, ny) * pcols, pcols)
        ready = p_t.at[own_ranks, at]
        send(ready, ready, fw_send, fw_recv, sibling)
        term = dot3(split(ready[...]), split(m_pair[at, :]), 1, 0)
        terms = term if terms is None else terms + term
    cross_out[...] = terms

    pair_at = lax.div(z, 2)
    for dz in ring:
        if dz % 2 == 0:
            send(cross_out, cross_in.at[pair_at], cross_send, cross_recv,
                 device(around(z, dz, nz), c, x, y))
    cross_in[pair_at] = terms

    await_bytes(from_core, fw_recv)
    gram = dot(p_t[...], p_t[...], 1, 1, highest)
    row_at = lax.broadcasted_iota(jnp.int32, (rank, rank), 0)
    col_at = lax.broadcasted_iota(jnp.int32, (rank, rank), 1)
    eye = jnp.where(row_at == col_at, 1.0, 0.0).astype(f32)
    trace = jnp.sum(jnp.sum(gram * eye, axis=1, keepdims=True), axis=0, keepdims=True)
    shift = ridge_scale * rows * (trace / (rows * rank) + 1e-05)
    table[...] = jnp.concatenate([gram + shift * eye, eye], axis=1)
    rank_at = lax.broadcasted_iota(jnp.int32, (rank, 1), 0)

    def eliminate(k, held):
        for j in range(8):
            row = held[j : j + 1, :]
            scale = held[:, j : j + 1] * (1.0 / row[:, j : j + 1])
            held = held - jnp.where((rank_at > j) & (rank_at < rank - 8 * k), scale, 0.0) * row
        held = jnp.concatenate([held[8:], held[:8]], axis=0)
        return pltpu.roll(held, 2 * rank - 8, 1)

    table[...] = lax.fori_loop(0, rank // 8, eliminate, table[...])

    await_bytes(cross_in.at[pl.ds(0, npair - 1)], cross_recv)
    place = odd * CORES + c
    n_all[place] = jnp.sum(cross_in[...], axis=0)
    for z_at, c_at in ((mate, 1 - c), (mate, c), (z, 1 - c)):
        send(n_all.at[place], n_all.at[place], back_send, back_recv, device(z_at, c_at, x, y))

    pivots = jnp.sum(table[:, rank:] * eye, axis=1, keepdims=True)
    inverse[...] = table[:, :rank] * (1.0 / jnp.sqrt(pivots))

    def transposed(k, carry):
        at = span(k * block, block)
        high, low = split(p_t[:, at].T)
        basis[at, :] = jnp.concatenate([high, low, high, jnp.zeros_like(high)], axis=1)
        return carry

    lax.fori_loop(0, rows // block, transposed, 0)

    await_bytes(n_all.at[pl.ds(0, 3)], back_recv)
    await_bytes(from_core, core_send)
    await_bytes(xy_in.at[pl.ds(0, arriving)], xy_send)
    await_bytes(m_core, m_send)
    await_bytes(z_in.at[pl.ds(0, nz - 1)], z_send)
    await_bytes(m_mate, mate_send)
    await_bytes(m_pair.at[pl.ds(0, half_rows), :], pair_send)
    await_bytes(xy_in.at[pl.ds(0, nt - 1)], ag_send)
    await_bytes(from_core, fw_send)
    await_bytes(cross_in.at[pl.ds(0, npair - 1)], cross_send)
    await_bytes(n_all.at[pl.ds(0, 3)], back_send)


def finish(replicas, merged, basis, n_all, inverse, factor_hbm, res_hbm, factor, res, sems):
    rows = merged.shape[0]
    terms = jnp.concatenate([
        jnp.concatenate([n_all[k], n_all[CORES + k]], axis=1) for k in range(CORES)
    ], axis=0)
    factor[...] = dot(inverse[...], terms, 1, 0, highest) * (1.0 / replicas)
    out = pltpu.make_async_copy(factor, factor_hbm, sems.at[0])
    out.start()
    outs = [out]
    high, low = split(dot(inverse[...], factor[...], 0, 0, highest))
    back = jnp.concatenate([high, high, low, jnp.zeros_like(low)], axis=0)
    step = rows // 4
    for k in range(4):
        at = pl.ds(k * step, step)
        res[at, :] = merged[at, :] - dot(basis[at, :], back, 1, 0)
        outs.append(pltpu.make_async_copy(res.at[at, :], res_hbm.at[0, at, :], sems.at[1 + k]))
        outs[-1].start()
    for out in outs:
        out.wait()


def on_device(nx, ny, nz, activations, out_grads, q_previous, carried_error):
    tokens, rows = activations.shape
    width = out_grads.shape[1]
    rank = q_previous.shape[0]
    half_rows = rows // CORES
    half_rank, half_width = rank // CORES, width // 2
    piece = (half_rank // nx, rows // ny)
    columns = (half_rows, half_width)
    terms = (half_rank, half_width)
    vmem, dma = pltpu.VMEM, pltpu.SemaphoreType.DMA
    anywhere = pl.BlockSpec(memory_space=pl.ANY)
    local = pl.BlockSpec(memory_space=pltpu.VMEM)
    in_hbm = [
        pltpu.with_memory_space_constraint(a, pltpu.HBM)
        for a in (activations, out_grads, q_previous, carried_error)
    ]
    passed = pl.pallas_call(
        functools.partial(kernel, nx, ny, nz),
        name="powersgd",
        out_shape=(
            vmem((rows, width), f32),
            vmem((rows, 4 * rank), bf16),
            vmem((4, *terms), f32),
            vmem((rank, rank), f32),
        ),
        in_specs=[anywhere] * 4,
        out_specs=(local,) * 4,
        scratch_shapes=[
            vmem((tokens, rows), bf16),
            vmem((tokens, width), bf16),
            vmem((rank, width), f32),
            vmem((rows, width), f32),
            vmem((rank, rows), f32),
            vmem((half_rank, rows), f32),
            vmem((half_rank, rows), f32),
            vmem((nx * ny + FAR[nx], *piece), f32),
            vmem(piece, f32),
            vmem((nz, *piece), f32),
            vmem((rank, rows), f32),
            vmem((half_rows, width), f32),
            vmem(columns, f32),
            vmem(columns, f32),
            vmem((rows, half_width), f32),
            vmem(terms, f32),
            vmem((nz // 2, *terms), f32),
            vmem((rank, 2 * rank), f32),
            dma((10,)),
            dma, dma,
            dma, dma,
            dma, dma,
            dma, dma((ny,)),
            dma, dma,
            dma, dma,
            dma, dma,
            dma, dma,
            dma, dma,
            dma, dma,
            pltpu.SemaphoreType.REGULAR((3,)),
        ],
        compiler_params=pltpu.CompilerParams(
            collective_id=0, has_side_effects=True, vmem_limit_bytes=20 * 1024 * 1024
        ),
    )(*in_hbm)
    return pl.pallas_call(
        functools.partial(finish, nz * CORES),
        name="residual",
        out_shape=(
            jax.ShapeDtypeStruct((rank, width), f32),
            jax.ShapeDtypeStruct((1, rows, width), f32),
        ),
        in_specs=[local] * 4,
        out_specs=(anywhere,) * 2,
        scratch_shapes=[vmem((rank, width), f32), vmem((rows, width), f32), dma((5,))],
        compiler_params=pltpu.CompilerParams(vmem_limit_bytes=16 * 1024 * 1024),
    )(*(pltpu.with_memory_space_constraint(a, pltpu.VMEM) for a in passed))


def solution(mesh):
    nz = mesh.shape["dp"] // CORES
    nx = ny = {16: 4, 4: 2}[mesh.shape["tensor"]]
    placed = (P("dp", None), P("dp", "tensor"), P(None, "tensor"), P("dp", None, "tensor"))
    return jax.shard_map(
        functools.partial(on_device, nx, ny, nz),
        mesh=mesh,
        in_specs=placed,
        out_specs=(P(None, "tensor"), P("dp", None, "tensor")),
        check_vma=False,
    )
```
